128 devices in a mesh: row: 8 (over x_lo, z), col: 16 (over x_hi, y, core).
Axes of the slice: x: 4 (x_hi: 2, x_lo: 2; x = x_hi * 2 + x_lo), y: 4, z: 4, core: 2. Of those that a mesh axis runs over, the one named last changes fastest.
Arguments:
- features: bfloat16 [65536, 256], P(('col', 'row'))
- weight: bfloat16 [256, 256], replicated, may hold values from -0.375 to 0.375
- tiles: bfloat16 [8, 16, 384, 128, 128], P('row', 'col'), may hold values from -0.0546875 to 0.0546875
- tile_coords: int32 [8, 16, 2, 384], P('row', 'col'), may hold values from 0 to 63, as said below
- tile_counts: int32 [8, 16], P('row', 'col'), may hold values from 48 to 384, as said below
- cotangent: bfloat16 [65536, 256], P(('row', 'col')), may hold values from -6 to 6
Outputs:
- output: bfloat16 [65536, 256], P(('row', 'col'))
- feature_grad: bfloat16 [65536, 256], P(('col', 'row'))
- weight_grad: float32 [256, 256], replicated
The draws below stay inside these ranges and needn't reach their ends.
Inputs may be any that keep to these rules, and one draw needn't show every extreme that they name: `tile_coords`: within one block the live and dead slots name distinct tiles; tile rows are below 64 and tile columns below 32. `tile_counts`: some block has all 384 slots live.
All inputs are finite; a program needn't handle non-finite values.
Results may differ from the reference program's by a relative error of at most 0.007.
Values may be sent and summed in bfloat16 or wider, within the bound.
A program may use at most 192 MiB of HBM per device.

```python
import jax
import jax.numpy as jnp
from jax import lax

FEAT = 256
TILE = 128
NODE_DEV = 512
MAXT = 384
NODES = 65536
TILE_ROWS = 64
TILE_COLS = 32
N_ROW = 8
N_COL = 16


def draw_features(key, part):
    key = jax.random.fold_in(key, 11)
    node_ids = jnp.arange(NODES, dtype=jnp.float32)
    rising = jnp.exp(jnp.log(3.0) * node_ids / NODES)[:, None]
    values = jax.random.normal(jax.random.fold_in(key, 1), (NODES, FEAT), jnp.float32) * rising
    return jnp.clip(values, -12.0, 12.0).astype(jnp.bfloat16)


def draw_tile_coords(key, part):
    key = jax.random.fold_in(key, 23)
    device_keys = jax.random.split(key, N_ROW * N_COL)
    chosen = jax.vmap(lambda single: jax.random.permutation(single, TILE_ROWS * TILE_COLS)[:MAXT])(device_keys)
    chosen = chosen.astype(jnp.int32)
    tile_rows = chosen // TILE_COLS
    tile_cols = chosen % TILE_COLS
    return jnp.stack([tile_rows, tile_cols], axis=1).reshape(N_ROW, N_COL, 2, MAXT)


def draw_tile_counts(key, part):
    key = jax.random.fold_in(key, 37)
    lowest = MAXT // 8
    span = MAXT - lowest
    first = jax.random.randint(jax.random.fold_in(key, 1), (N_ROW * N_COL,), 0, span + 1)
    second = jax.random.randint(jax.random.fold_in(key, 2), (N_ROW * N_COL,), 0, span + 1)
    counts = lowest + first * second // span
    busiest = jax.random.randint(jax.random.fold_in(key, 3), (), 0, N_ROW * N_COL)
    counts = jnp.where(jnp.arange(N_ROW * N_COL) == busiest, MAXT, counts)
    return counts.astype(jnp.int32).reshape(N_ROW, N_COL)


def level_of(stream_key, shape, shards, least, high):
    def one(dim, shards_of):
        heights = jax.random.uniform(jax.random.fold_in(jax.random.fold_in(stream_key, 6), dim), (shards_of,), jnp.float32, least / len(shards), high / len(shards))
        return jnp.repeat(jnp.exp(heights), shape[dim] // shards_of).reshape((-1,) + (1,) * (len(shape) - dim - 1))

    gain = one(*shards[0])
    for cut in shards[1:]:
        gain = gain * one(*cut)
    return gain


def normal_values(key, shape, width, bound, shards=(), kind=jnp.bfloat16):
    entries = jax.random.normal(key, shape, jnp.float32) * width
    if len(shards) > 0:
        entries = level_of(key, shape, shards, -0.22, 0.18) * entries
    return jnp.clip(entries, min=-bound, max=bound).astype(kind)


def setup_inputs(seed: int = 0) -> dict:
    streams_of = jax.random.split(jax.random.key(seed), 7)
    return {
        "features": draw_features(jax.random.fold_in(streams_of[6], 71), 0),
        "weight": normal_values(streams_of[1], (FEAT, FEAT), FEAT ** -0.5, 0.375),
        "tiles": normal_values(streams_of[2], (N_ROW, N_COL, MAXT, TILE, TILE), (TILE * TILE * MAXT // NODE_DEV) ** -0.5, 0.0546875, ((0, 8), (1, 16))),
        "tile_coords": draw_tile_coords(jax.random.fold_in(streams_of[6], 71), 0),
        "tile_counts": draw_tile_counts(jax.random.fold_in(streams_of[6], 71), 0),
        "cotangent": normal_values(streams_of[5], (NODES, FEAT), 1.0, 6.0, ((0, 128),)),
    }


def local_product(tile_block, tile_rows, tile_cols, live_count, panel_tiles, out_count, transpose):
    block = min(128, tile_block.shape[0])
    blocks_total = tile_block.shape[0] // block

    def step(index, running):
        start = index * block
        values = lax.dynamic_slice_in_dim(tile_block, start, block, 0).astype(jnp.float32)
        rows_here = lax.dynamic_slice_in_dim(tile_rows, start, block, 0)
        cols_here = lax.dynamic_slice_in_dim(tile_cols, start, block, 0)
        slot_ids = start + jnp.arange(block, dtype=jnp.int32)
        live = slot_ids < live_count
        if transpose:
            source = panel_tiles[rows_here].astype(jnp.float32)
            product = jnp.einsum("tab,taf->tbf", values, source)
            target = cols_here
        else:
            source = panel_tiles[cols_here].astype(jnp.float32)
            product = jnp.einsum("tab,tbf->taf", values, source)
            target = rows_here
        product = jnp.where(live[:, None, None], product, 0.0)
        return running + jax.ops.segment_sum(product, target, num_segments=out_count)

    start_value = jnp.zeros((out_count, panel_tiles.shape[1], panel_tiles.shape[2]), jnp.float32)
    return lax.fori_loop(0, blocks_total, step, start_value)


def reference(features, weight, tiles, tile_coords, tile_counts, cotangent):
    projected = jnp.dot(features, weight, preferred_element_type=jnp.float32).astype(jnp.bfloat16)
    col_panels = projected.reshape(N_COL, TILE_COLS, TILE, FEAT)

    def forward_step(flat_index, running):
        row_id = flat_index // N_COL
        col_id = flat_index % N_COL
        part = local_product(tiles[row_id, col_id], tile_coords[row_id, col_id, 0], tile_coords[row_id, col_id, 1],
                             tile_counts[row_id, col_id], col_panels[col_id], TILE_ROWS, False)
        return running.at[row_id].add(part)

    hidden = lax.fori_loop(0, N_ROW * N_COL, forward_step,
                           jnp.zeros((N_ROW, TILE_ROWS, TILE, FEAT), jnp.float32)).reshape(NODES, FEAT)
    sigma = jax.nn.sigmoid(hidden)
    output = (hidden * sigma).astype(jnp.bfloat16)
    hidden_grad = (cotangent.astype(jnp.float32) * sigma * (1.0 + hidden * (1.0 - sigma))).astype(jnp.bfloat16)
    row_panels = hidden_grad.reshape(N_ROW, TILE_ROWS, TILE, FEAT)

    def backward_step(flat_index, running):
        row_id = flat_index // N_COL
        col_id = flat_index % N_COL
        part = local_product(tiles[row_id, col_id], tile_coords[row_id, col_id, 0], tile_coords[row_id, col_id, 1],
                             tile_counts[row_id, col_id], row_panels[row_id], TILE_COLS, True)
        return running.at[col_id].add(part)

    projected_grad = lax.fori_loop(0, N_ROW * N_COL, backward_step,
                                   jnp.zeros((N_COL, TILE_COLS, TILE, FEAT), jnp.float32))
    projected_grad = projected_grad.reshape(NODES, FEAT).astype(jnp.bfloat16)
    feature_grad = jnp.dot(projected_grad, weight.T, preferred_element_type=jnp.float32).astype(jnp.bfloat16)
    weight_grad = jnp.dot(features.T, projected_grad, preferred_element_type=jnp.float32)
    return output, feature_grad, weight_grad
```

```python
import functools

import jax
import jax.numpy as jnp
from jax import lax
from jax.experimental import pallas as pl
from jax.experimental.pallas import tpu as pltpu
from jax.sharding import PartitionSpec as P

MESH = pl.DeviceIdType.MESH
BF = jnp.bfloat16
F32 = jnp.float32
ANY = pl.BlockSpec(memory_space=pl.ANY)
VMEM = pl.BlockSpec(memory_space=pltpu.VMEM)
SMEM = pl.BlockSpec(memory_space=pltpu.SMEM)
VMEM_BYTES = 60 * 2**20
SIDE = 128
FEAT = 256
SLOTS = 384
CHUNK = 32
H = (pl.ds(0, 2), pl.ds(2, 2))


class Group:
    def __init__(self, along):
        row = lax.axis_index("row")
        col = lax.axis_index("col")
        if along == "row":
            place = row
            self.device = lambda g: (g, col)
        else:
            place = lax.div(col, 2)
            core = lax.rem(col, 2)
            self.device = lambda g: (row, g * 2 + core)
            self.sibling = (row, place * 2 + 1 - core)
            self.core = core
        a = lax.div(place, 4)
        b = lax.rem(place, 4)
        up = lax.rem(b + 1, 4)
        down = lax.rem(b + 3, 4)
        far = lax.rem(b + 2, 4)
        self.own = place
        self.up, self.down, self.far = a * 4 + up, a * 4 + down, a * 4 + far
        self.other = (1 - a) * 4 + b
        self.other_up, self.other_down, self.other_far = (
            (1 - a) * 4 + up,
            (1 - a) * 4 + down,
            (1 - a) * 4 + far,
        )

    def peers(self):
        return [self.device(g) for g in (self.up, self.down, self.far, self.other)]


def greet(peers):
    barrier = pltpu.get_barrier_semaphore()
    for peer in peers:
        pl.semaphore_signal(barrier, inc=1, device_id=peer, device_id_type=MESH)
    pl.semaphore_wait(barrier, len(peers))


def ring_sum(group, send, whole, size, got, met, out, base):
    rows = lambda b: pl.ds(b * size, size)
    ring = [(group.device(g), lax.rem(g, 4)) for g in (group.up, group.down, group.far)]
    mine = lax.rem(group.own, 4)
    copies = [send(whole.at[rows(b)], got.at[k], peer) for k, (peer, b) in enumerate(ring)]
    yield
    for copy in copies:
        copy.wait_recv()
    met[0] = whole[rows(mine)] + got[0] + got[1] + got[2]
    copy = send(met.at[0], met.at[1], group.device(group.other))
    yield
    copy.wait_recv()
    spot = out.at[pl.ds(base + mine * size, size)]
    spot[...] = met[0] + met[1]
    copies = [send(spot, spot, peer) for peer, _ in ring]
    yield
    for copy in copies:
        copy.wait_recv()


def pair_then_ring_sum(group, send, whole, theirs, half, got, met, out):
    size = whole.shape[0] // 2
    mine = pl.ds(group.core * size, size)
    copy = send(whole.at[pl.ds((1 - group.core) * size, size)], theirs, group.sibling)
    yield
    copy.wait_recv()
    half[...] = whole[mine] + theirs[...]
    yield from ring_sum(group, send, half, size // 4, got, met, out, group.core * size)
    copy = send(out.at[mine], out.at[mine], group.sibling)
    yield
    copy.wait_recv()


class Sender:
    def __init__(self, send_sem, recv_sem):
        self.send_sem, self.recv_sem = send_sem, recv_sem
        self.used = 0
        self.all = []

    def __call__(self, src, dst, device):
        copy = pltpu.make_async_remote_copy(
            src_ref=src,
            dst_ref=dst,
            send_sem=self.send_sem.at[self.used],
            recv_sem=self.recv_sem.at[self.used],
            device_id=device,
            device_id_type=MESH,
        )
        self.used += 1
        self.all.append(copy)
        copy.start()
        return copy

    def finish(self):
        for copy in self.all:
            copy.wait_send()


def gather(group, send, own, spot, landed, tick=lambda: None):
    up, down, other = (group.device(g) for g in (group.up, group.down, group.other))
    here = spot(group.own)
    c_up, c_down, c_other = [None, None], [None, None], [None, None]
    for h in (0, 1):
        c_up[h] = send(own.at[H[h]], here.at[H[h]], up)
        c_down[1 - h] = send(own.at[H[1 - h]], here.at[H[1 - h]], down)
        c_other[h] = send(own.at[H[h]], here.at[H[h]], other)
    tick()
    f_up, f_down = [None, None], [None, None]
    c_up[0].wait_recv()
    far_first = send(spot(group.down).at[H[0]], spot(group.down).at[H[0]], up)
    landed(group.down, 0)
    c_down[1].wait_recv()
    far_second = send(spot(group.up).at[H[1]], spot(group.up).at[H[1]], down)
    landed(group.up, 1)
    for h in (0, 1):
        c_other[h].wait_recv()
        block = spot(group.other).at[H[h]]
        f_up[h] = send(block, block, up)
        f_down[h] = send(block, block, down)
        landed(group.other, h)
    tick()
    c_up[1].wait_recv()
    landed(group.down, 1)
    c_down[0].wait_recv()
    landed(group.up, 0)
    far_first.wait_recv()
    block = spot(group.far).at[H[0]]
    x_first = send(block, block, other)
    landed(group.far, 0)
    far_second.wait_recv()
    block = spot(group.far).at[H[1]]
    x_second = send(block, block, other)
    landed(group.far, 1)
    tick()
    for h in (0, 1):
        f_up[h].wait_recv()
        landed(group.other_down, h)
        f_down[h].wait_recv()
        landed(group.other_up, h)
    x_first.wait_recv()
    landed(group.other_far, 0)
    x_second.wait_recv()
    landed(group.other_far, 1)


def plus(target, *terms):
    total = terms[0][...].astype(F32)
    for term in terms[1:]:
        total = total + term[...].astype(F32)
    target[...] = total.astype(target.dtype)


def scatter_sum(group, send, ready, spot, got, tick=lambda: None):
    r1, r2d, r2u, r3, r4d, r4u, r5 = (got.at[k] for k in range(7))
    up, down, other = (group.device(g) for g in (group.up, group.down, group.other))
    ready(group.other_far)
    c1 = [send(spot(group.other_far).at[H[h]], r1.at[H[h]], other) for h in (0, 1)]
    ready(group.other_up)
    c2u = [send(spot(group.other_up).at[H[h]], r2d.at[H[h]], up) for h in (0, 1)]
    ready(group.other_down)
    c2d = [send(spot(group.other_down).at[H[h]], r2u.at[H[h]], down) for h in (0, 1)]
    ready(group.up)
    c4u, c4d = [None, None], [None, None]
    c4u[1] = send(spot(group.up).at[H[1]], r4d.at[H[1]], up)
    ready(group.down)
    c4d[0] = send(spot(group.down).at[H[0]], r4u.at[H[0]], down)
    ready(group.far)
    tick()
    c1[0].wait_recv()
    plus(r1.at[H[0]], r1.at[H[0]], spot(group.far).at[H[0]])
    c3u = send(r1.at[H[0]], r3.at[H[0]], up)
    tick()
    c1[1].wait_recv()
    plus(r1.at[H[1]], r1.at[H[1]], spot(group.far).at[H[1]])
    c3d = send(r1.at[H[1]], r3.at[H[1]], down)
    ready(group.other)
    tick()
    c5 = []
    for h in (0, 1):
        c2u[h].wait_recv()
        c2d[h].wait_recv()
        plus(r2d.at[H[h]], r2d.at[H[h]], r2u.at[H[h]], spot(group.other).at[H[h]])
        c5.append(send(r2d.at[H[h]], r5.at[H[h]], other))
        tick()
    c3u.wait_recv()
    plus(r3.at[H[0]], r3.at[H[0]], spot(group.up).at[H[0]])
    c4u[0] = send(r3.at[H[0]], r4d.at[H[0]], up)
    c3d.wait_recv()
    plus(r3.at[H[1]], r3.at[H[1]], spot(group.down).at[H[1]])
    c4d[1] = send(r3.at[H[1]], r4u.at[H[1]], down)
    ready(group.own)
    for copies in (c5, c4u, c4d):
        for copy in copies:
            copy.wait_recv()
    return (spot(group.own), r4d, r4u, r5)


def gather_features(own_ref, out_ref, send_sem, recv_sem, local_sem):
    group = Group("row")
    greet([group.device(g) for g in (group.up, group.down, group.other)])
    send = Sender(send_sem, recv_sem)
    mine = pltpu.make_async_copy(own_ref, out_ref.at[group.own], local_sem)
    mine.start()
    gather(group, send, own_ref, lambda g: out_ref.at[g], lambda g, h: None)
    mine.wait()
    send.finish()


def tile_sums(transpose, coords, count_ref, panel_hbm, tiles_hbm, out_hbm, tiles, panel, acc, out, sems):
    count = count_ref[0, 0]
    panel_copy = pltpu.make_async_copy(panel_hbm, panel, sems.at[0])
    panel_copy.start()
    chunks = SLOTS // CHUNK

    def fetch(k):
        part = pl.ds(k * CHUNK, CHUNK)
        return pltpu.make_async_copy(tiles_hbm.at[part], tiles.at[part], sems.at[k + 1])

    def begin(k, _):
        @pl.when(k * CHUNK < count)
        def _():
            fetch(k).start()

        return 0

    lax.fori_loop(0, chunks, begin, 0)
    outs = out.shape[0]

    def clear(k, _):
        acc[k] = jnp.zeros(acc.shape[1:], F32)
        return 0

    lax.fori_loop(0, outs, clear, 0)
    panel_copy.wait()
    unroll = 8

    def step(s):
        row, column = coords[0, s], coords[1, s]
        source, target = (row, column) if transpose else (column, row)
        target = jnp.where(s < count, target, outs)
        if transpose:
            product = jnp.dot(panel[source], tiles[s], preferred_element_type=F32)
        else:
            product = jnp.dot(tiles[s], panel[source], preferred_element_type=F32)
        acc[target] += product

    def chunk(k, _):
        @pl.when(k * CHUNK < count)
        def _():
            fetch(k).wait()

            def several(i, _):
                for u in range(unroll):
                    step(k * CHUNK + i * unroll + u)
                return 0

            left = jnp.minimum(count - k * CHUNK, CHUNK)
            lax.fori_loop(0, lax.div(left + unroll - 1, unroll), several, 0)

        return 0

    lax.fori_loop(0, chunks, chunk, 0)
    parts = 4
    size = outs // parts
    copies = []
    for p in range(parts):

        def narrow(k, _):
            out[k] = acc[k].astype(BF)
            return 0

        lax.fori_loop(p * size, (p + 1) * size, narrow, 0)
        part = pl.ds(p * size, size)
        copy = pltpu.make_async_copy(out.at[part], out_hbm.at[part], sems.at[chunks + 1 + p])
        copy.start()
        copies.append(copy)
    for copy in copies:
        copy.wait()


def middle(
    part_hbm, weight, cotangent, output, grads, weight_grad,
    part, theirs, got, total_hi, total_lo, own, whole, ring_got, ring_met, send_sem, recv_sem, local_sem,
):
    group = Group("col")
    rows_group = Group("row")
    core = group.core
    load = pltpu.make_async_copy(part_hbm, part, local_sem)
    load.start()
    greet([group.device(g) for g in (group.up, group.down, group.other)] + [group.sibling] + rows_group.peers())
    send = Sender(send_sem, recv_sem)
    order = (
        group.other_far, group.other_up, group.other_down, group.up,
        group.down, group.far, group.other, group.own,
    )
    pairs = []
    for k, g in enumerate(order):
        source = part_hbm.at[pl.ds((g * 2 + 1 - core) * 4, 4)]
        pairs.append(send(source, theirs.at[k], group.sibling))
    load.wait()
    step = iter(range(len(order)))
    held = {}

    def ready(g):
        k = next(step)
        pairs[k].wait_recv()
        held[id(g)] = k
        mine = part.at[pl.ds((g * 2 + core) * 4, 4)]
        for h in (0, 1):
            plus(theirs.at[k, H[h]], theirs.at[k, H[h]], mine.at[H[h]])

    terms = scatter_sum(group, send, ready, lambda g: theirs.at[held[id(g)]], got)
    for t in range(4):
        total = terms[0][t].astype(F32)
        for term in terms[1:]:
            total = total + term[t].astype(F32)
        rows = pl.ds(t * SIDE, SIDE)
        high = total.astype(BF)
        low = (total - high.astype(F32)).astype(BF)
        total_hi[rows] = high
        total_lo[rows] = low
        hidden = jnp.dot(high, weight[...], preferred_element_type=F32) + jnp.dot(
            low, weight[...], preferred_element_type=F32
        )
        sigma = 1.0 / (1.0 + jnp.exp(-hidden))
        output[rows] = (hidden * sigma).astype(BF)
        slope = (cotangent[rows].astype(F32) * sigma * (1.0 + hidden * (1.0 - sigma))).astype(BF)
        own[rows] = slope
        grads[group.own * 8 + core * 4 + t] = lax.dot_general(
            weight[...], slope, (((1,), (1,)), ((), ())), preferred_element_type=F32
        ).astype(BF)

    def spot(g):
        return grads.at[pl.ds((g * 2 + core) * 4, 4)]

    def landed(g, h):
        block = spot(g).at[H[h]]
        back.append(send(block, block, group.sibling))

    back = []
    landed(group.own, 0)
    landed(group.own, 1)

    def weight_sum():
        over = (((0,), (0,)), ((), ()))
        whole[...] = lax.dot_general(
            total_hi[...], own[...], over, preferred_element_type=F32
        ) + lax.dot_general(total_lo[...], own[...], over, preferred_element_type=F32)
        yield from ring_sum(rows_group, send, whole, FEAT // 4, ring_got, ring_met, weight_grad, 0)

    stages = weight_sum()
    gather(group, send, spot(group.own), spot, landed, lambda: next(stages, None))
    for _ in stages:
        pass
    for copy in back:
        copy.wait_recv()
    send.finish()


def last_sum(part, weight_part, out, weight_grad, got, theirs, half, ring_got, ring_met, send_sem, recv_sem):
    group = Group("row")
    cols_group = Group("col")
    greet([group.device(g) for g in (group.up, group.down, group.other)] + [cols_group.sibling] + cols_group.peers())
    send = Sender(send_sem, recv_sem)
    stages = pair_then_ring_sum(cols_group, send, weight_part, theirs, half, ring_got, ring_met, weight_grad)
    terms = scatter_sum(
        group, send, lambda g: None, lambda g: part.at[pl.ds(g * 4, 4)], got, lambda: next(stages, None)
    )
    for _ in stages:
        pass
    for t in range(4):
        total = terms[0][t].astype(F32)
        for term in terms[1:]:
            total = total + term[t].astype(F32)
        out[pl.ds(t * SIDE, SIDE)] = total.T.astype(BF)
    send.finish()


def params(collective_id=None):
    if collective_id is None:
        return pltpu.CompilerParams(vmem_limit_bytes=VMEM_BYTES)
    return pltpu.CompilerParams(
        collective_id=collective_id, has_side_effects=True, vmem_limit_bytes=VMEM_BYTES
    )


def sems(n):
    return [pltpu.SemaphoreType.DMA((n,)), pltpu.SemaphoreType.DMA((n,))]


def run_tiles(transpose, coords, count, panel, tiles):
    outs = 32 if transpose else 64
    ins = 64 if transpose else 32
    block = (FEAT, SIDE) if transpose else (SIDE, FEAT)
    return pl.pallas_call(
        functools.partial(tile_sums, transpose),
        out_shape=jax.ShapeDtypeStruct((outs,) + block, BF),
        in_specs=[SMEM, SMEM, ANY, ANY],
        out_specs=ANY,
        scratch_shapes=[
            pltpu.VMEM((SLOTS, SIDE, SIDE), BF),
            pltpu.VMEM((ins,) + block, BF),
            pltpu.VMEM((outs + 1,) + block, F32),
            pltpu.VMEM((outs,) + block, BF),
            pltpu.SemaphoreType.DMA((SLOTS // CHUNK + 5,)),
        ],
        compiler_params=params(),
        name="tiles_back" if transpose else "tiles_forward",
    )(coords, count, panel, tiles)


def run_gather(features):
    return pl.pallas_call(
        gather_features,
        out_shape=jax.ShapeDtypeStruct((8, 4, SIDE, FEAT), BF),
        in_specs=[VMEM],
        out_specs=VMEM,
        scratch_shapes=sems(14) + [pltpu.SemaphoreType.DMA],
        compiler_params=params(0),
        name="gather_features",
    )(features.reshape(4, SIDE, FEAT))


def run_middle(part, weight, cotangent):
    nodes = 4 * SIDE
    return pl.pallas_call(
        middle,
        out_shape=(
            jax.ShapeDtypeStruct((nodes, FEAT), BF),
            jax.ShapeDtypeStruct((64, FEAT, SIDE), BF),
            jax.ShapeDtypeStruct((FEAT, FEAT), F32),
        ),
        in_specs=[ANY, VMEM, VMEM],
        out_specs=(VMEM, VMEM, VMEM),
        scratch_shapes=[
            pltpu.VMEM((64, SIDE, FEAT), BF),
            pltpu.VMEM((8, 4, SIDE, FEAT), BF),
            pltpu.VMEM((7, 4, SIDE, FEAT), BF),
            pltpu.VMEM((nodes, FEAT), BF),
            pltpu.VMEM((nodes, FEAT), BF),
            pltpu.VMEM((nodes, FEAT), BF),
            pltpu.VMEM((FEAT, FEAT), F32),
            pltpu.VMEM((3, FEAT // 4, FEAT), F32),
            pltpu.VMEM((2, FEAT // 4, FEAT), F32),
        ]
        + sems(59)
        + [pltpu.SemaphoreType.DMA],
        compiler_params=params(1),
        name="middle",
    )(part, weight, cotangent)


def run_last(part, weight_part):
    return pl.pallas_call(
        last_sum,
        out_shape=(
            jax.ShapeDtypeStruct((4 * SIDE, FEAT), BF),
            jax.ShapeDtypeStruct((FEAT, FEAT), F32),
        ),
        in_specs=[VMEM, VMEM],
        out_specs=(VMEM, VMEM),
        scratch_shapes=[
            pltpu.VMEM((7, 4, FEAT, SIDE), BF),
            pltpu.VMEM((FEAT // 2, FEAT), F32),
            pltpu.VMEM((FEAT // 2, FEAT), F32),
            pltpu.VMEM((3, FEAT // 8, FEAT), F32),
            pltpu.VMEM((2, FEAT // 8, FEAT), F32),
        ]
        + sems(23),
        compiler_params=params(2),
        name="last_sum",
    )(part, weight_part)


def local(features, weight, tiles, tile_coords, tile_counts, cotangent):
    my_tiles, coords = tiles[0, 0], tile_coords[0, 0]
    panel = run_gather(features).reshape(32, SIDE, FEAT)
    part = run_tiles(False, coords, tile_counts, panel, my_tiles)
    output, grads, local_weight_grad = run_middle(part, weight, cotangent)
    back = run_tiles(True, coords, tile_counts, grads, my_tiles)
    feature_grad, weight_grad = run_last(back, local_weight_grad)
    return (output, feature_grad, weight_grad)


def solution(mesh):
    placed = (
        P(("col", "row"), None),
        P(),
        P("row", "col", None, None, None),
        P("row", "col", None, None),
        P("row", "col"),
        P(("row", "col"), None),
    )
    return jax.shard_map(
        local,
        mesh=mesh,
        in_specs=placed,
        out_specs=(P(("row", "col"), None), P(("col", "row"), None), P()),
        check_vma=False,
    )
```

```python
import functools

import jax
import jax.numpy as jnp
from jax import lax
from jax.experimental import pallas as pl
from jax.experimental.pallas import tpu as pltpu
from jax.sharding import PartitionSpec as P

MESH = pl.DeviceIdType.MESH
BF = jnp.bfloat16
F32 = jnp.float32
ANY = pl.BlockSpec(memory_space=pl.ANY)
VMEM = pl.BlockSpec(memory_space=pltpu.VMEM)
SMEM = pl.BlockSpec(memory_space=pltpu.SMEM)
VMEM_BYTES = 60 * 2**20
SIDE = 128
FEAT = 256
SLOTS = 384
PAIRS_FORWARD = (SLOTS + 64) // 2
PAIRS_BACK = (SLOTS + 32) // 2
UNROLL = 8
PLACES = 512
H = (pl.ds(0, 2), pl.ds(2, 2))


class Group:
    def __init__(self, along):
        row = lax.axis_index("row")
        col = lax.axis_index("col")
        if along == "row":
            place = row
            self.device = lambda g: (g, col)
        else:
            place = lax.div(col, 2)
            core = lax.rem(col, 2)
            self.device = lambda g: (row, g * 2 + core)
            self.sibling = (row, place * 2 + 1 - core)
            self.core = core
        a = lax.div(place, 4)
        b = lax.rem(place, 4)
        up = lax.rem(b + 1, 4)
        down = lax.rem(b + 3, 4)
        far = lax.rem(b + 2, 4)
        self.own = place
        self.up, self.down, self.far = a * 4 + up, a * 4 + down, a * 4 + far
        self.other = (1 - a) * 4 + b
        self.other_up, self.other_down, self.other_far = (
            (1 - a) * 4 + up,
            (1 - a) * 4 + down,
            (1 - a) * 4 + far,
        )

    def peers(self):
        return [self.device(g) for g in (self.up, self.down, self.far, self.other)]


def greet(peers):
    barrier = pltpu.get_barrier_semaphore()
    for peer in peers:
        pl.semaphore_signal(barrier, inc=1, device_id=peer, device_id_type=MESH)
    pl.semaphore_wait(barrier, len(peers))


def ring_sum(group, send, whole, size, got, met, out, base):
    rows = lambda b: pl.ds(b * size, size)
    ring = [(group.device(g), lax.rem(g, 4)) for g in (group.up, group.down, group.far)]
    mine = lax.rem(group.own, 4)
    copies = [send(whole.at[rows(b)], got.at[k], peer) for k, (peer, b) in enumerate(ring)]
    yield
    for copy in copies:
        copy.wait_recv()
    met[0] = whole[rows(mine)] + got[0] + got[1] + got[2]
    copy = send(met.at[0], met.at[1], group.device(group.other))
    yield
    copy.wait_recv()
    spot = out.at[pl.ds(base + mine * size, size)]
    spot[...] = met[0] + met[1]
    copies = [send(spot, spot, peer) for peer, _ in ring]
    yield
    for copy in copies:
        copy.wait_recv()


def pair_then_ring_sum(group, send, whole, theirs, half, got, met, out):
    size = whole.shape[0] // 2
    mine = pl.ds(group.core * size, size)
    copy = send(whole.at[pl.ds((1 - group.core) * size, size)], theirs, group.sibling)
    yield
    copy.wait_recv()
    half[...] = whole[mine] + theirs[...]
    yield from ring_sum(group, send, half, size // 4, got, met, out, group.core * size)
    copy = send(out.at[mine], out.at[mine], group.sibling)
    yield
    copy.wait_recv()


class Sender:
    def __init__(self, send_sem, recv_sem):
        self.send_sem, self.recv_sem = send_sem, recv_sem
        self.used = 0
        self.all = []

    def __call__(self, src, dst, device):
        copy = pltpu.make_async_remote_copy(
            src_ref=src,
            dst_ref=dst,
            send_sem=self.send_sem.at[self.used],
            recv_sem=self.recv_sem.at[self.used],
            device_id=device,
            device_id_type=MESH,
        )
        self.used += 1
        self.all.append(copy)
        copy.start()
        return copy

    def finish(self):
        for copy in self.all:
            copy.wait_send()


def gather(group, send, own, spot, landed, tick=lambda: None):
    up, down, other = (group.device(g) for g in (group.up, group.down, group.other))
    here = spot(group.own)
    c_up, c_down, c_other = [None, None], [None, None], [None, None]
    for h in (0, 1):
        c_up[h] = send(own.at[H[h]], here.at[H[h]], up)
        c_down[1 - h] = send(own.at[H[1 - h]], here.at[H[1 - h]], down)
        c_other[h] = send(own.at[H[h]], here.at[H[h]], other)
    tick()
    f_up, f_down = [None, None], [None, None]
    c_up[0].wait_recv()
    far_first = send(spot(group.down).at[H[0]], spot(group.down).at[H[0]], up)
    landed(group.down, 0)
    c_down[1].wait_recv()
    far_second = send(spot(group.up).at[H[1]], spot(group.up).at[H[1]], down)
    landed(group.up, 1)
    for h in (0, 1):
        c_other[h].wait_recv()
        block = spot(group.other).at[H[h]]
        f_up[h] = send(block, block, up)
        f_down[h] = send(block, block, down)
        landed(group.other, h)
    tick()
    c_up[1].wait_recv()
    landed(group.down, 1)
    c_down[0].wait_recv()
    landed(group.up, 0)
    far_first.wait_recv()
    block = spot(group.far).at[H[0]]
    x_first = send(block, block, other)
    landed(group.far, 0)
    far_second.wait_recv()
    block = spot(group.far).at[H[1]]
    x_second = send(block, block, other)
    landed(group.far, 1)
    tick()
    for h in (0, 1):
        f_up[h].wait_recv()
        landed(group.other_down, h)
        f_down[h].wait_recv()
        landed(group.other_up, h)
    x_first.wait_recv()
    landed(group.other_far, 0)
    x_second.wait_recv()
    landed(group.other_far, 1)


def plus(target, *terms):
    total = terms[0][...].astype(F32)
    for term in terms[1:]:
        total = total + term[...].astype(F32)
    target[...] = total.astype(target.dtype)


def scatter_sum(group, send, ready, spot, got, tick=lambda: None):
    r1, r2d, r2u, r3, r4d, r4u, r5 = (got.at[k] for k in range(7))
    up, down, other = (group.device(g) for g in (group.up, group.down, group.other))
    ready(group.other_far)
    c1 = [send(spot(group.other_far).at[H[h]], r1.at[H[h]], other) for h in (0, 1)]
    ready(group.other_up)
    c2u = [send(spot(group.other_up).at[H[h]], r2d.at[H[h]], up) for h in (0, 1)]
    ready(group.other_down)
    c2d = [send(spot(group.other_down).at[H[h]], r2u.at[H[h]], down) for h in (0, 1)]
    ready(group.up)
    c4u, c4d = [None, None], [None, None]
    c4u[1] = send(spot(group.up).at[H[1]], r4d.at[H[1]], up)
    ready(group.down)
    c4d[0] = send(spot(group.down).at[H[0]], r4u.at[H[0]], down)
    ready(group.far)
    tick()
    c1[0].wait_recv()
    plus(r1.at[H[0]], r1.at[H[0]], spot(group.far).at[H[0]])
    c3u = send(r1.at[H[0]], r3.at[H[0]], up)
    tick()
    c1[1].wait_recv()
    plus(r1.at[H[1]], r1.at[H[1]], spot(group.far).at[H[1]])
    c3d = send(r1.at[H[1]], r3.at[H[1]], down)
    ready(group.other)
    tick()
    c5 = []
    for h in (0, 1):
        c2u[h].wait_recv()
        c2d[h].wait_recv()
        plus(r2d.at[H[h]], r2d.at[H[h]], r2u.at[H[h]], spot(group.other).at[H[h]])
        c5.append(send(r2d.at[H[h]], r5.at[H[h]], other))
        tick()
    c3u.wait_recv()
    plus(r3.at[H[0]], r3.at[H[0]], spot(group.up).at[H[0]])
    c4u[0] = send(r3.at[H[0]], r4d.at[H[0]], up)
    c3d.wait_recv()
    plus(r3.at[H[1]], r3.at[H[1]], spot(group.down).at[H[1]])
    c4d[1] = send(r3.at[H[1]], r4u.at[H[1]], down)
    ready(group.own)
    for copies in (c5, c4u, c4d):
        for copy in copies:
            copy.wait_recv()
    return (spot(group.own), r4d, r4u, r5)


def pair_list(key, source, live, outs, empty, pairs):
    def iota(shape, dim):
        return lax.broadcasted_iota(jnp.int32, shape, dim)

    def add(x, axis):
        return jnp.sum(x, axis=axis, keepdims=True, dtype=jnp.int32)

    def upright(x):
        n = x.shape[1]
        return add(jnp.where(iota((n, n), 0) == iota((n, n), 1), x, 0), 1)

    key_up, source_up, live_up = upright(key), upright(source), upright(live)
    square = (SLOTS, SLOTS)
    before = (key_up == key) & (iota(square, 1) < iota(square, 0))
    rank = add(jnp.where(before, live, 0), 1)
    member = jnp.where(key_up == iota((SLOTS, SIDE), 1), live_up, 0)
    held = (add(member, 0) + 1) >> 1
    tri = (SIDE, SIDE)
    start = add(jnp.where(iota(tri, 0) < iota(tri, 1), upright(held), 0), 0)
    place = jnp.where(live_up > 0, 2 * add(member * start, 1) + rank, -1)
    wide = (SLOTS, PLACES)
    hit = place == iota(wide, 1)
    slots = add(jnp.where(hit, iota(wide, 0), 0), 0)
    sources = add(jnp.where(hit, source_up - empty, 0), 0) + empty
    firsts = add(jnp.where(hit & (rank == 0), 1, 0), 0)
    last = jnp.where(held > 0, start + held - 1, pairs)
    last = jnp.concatenate([last, jnp.zeros((1, PLACES - SIDE), jnp.int32)], axis=1)
    row = iota((8, PLACES), 0)
    return jnp.where(row == 0, slots, jnp.where(row == 1, sources, jnp.where(row == 2, firsts, last)))


def tile_sums(transpose, table, tiles, panel, sums, pairs):
    block = sums.shape[1:]
    sums[pairs] = jnp.zeros(block, BF)

    def several(i, run):
        for u in range(UNROLL):
            q = i * UNROLL + u
            values = [tiles[table[0, 2 * q + k]] for k in (0, 1)]
            sources = [panel[table[1, 2 * q + k]] for k in (0, 1)]
            if transpose:
                left, right = jnp.concatenate(sources, 1), jnp.concatenate(values, 0)
            else:
                left, right = jnp.concatenate(values, 1), jnp.concatenate(sources, 0)
            run = jnp.where(table[2, 2 * q] == 1, 0.0, run)
            run = run + jnp.dot(left, right, preferred_element_type=F32)
            sums[q] = run.astype(BF)
        return run

    lax.fori_loop(0, pairs // UNROLL, several, jnp.zeros(block, F32))


def layer(
    features, weight_hbm, tiles_hbm, coords, count, cotangent_hbm,
    output_hbm, feature_hbm, weight_grad,
    tiles, panel, grads, sums_forward, sums_back, given, theirs, back, got_forward, got_back,
    lists, table_forward, table_back, weight, cotangent, output, feature_grad,
    total_hi, total_lo, own, whole, row_sum, row_got, row_met, half, half_got, col_got, col_met,
    send_sem, recv_sem, load_sem, tile_sem,
):
    rows_group, cols_group = Group("row"), Group("col")
    core, sibling = cols_group.core, cols_group.sibling
    greet(rows_group.peers() + cols_group.peers() + [sibling])
    send = Sender(send_sem, recv_sem)
    loads = [
        pltpu.make_async_copy(features, panel.at[pl.ds(rows_group.own * 4, 4)], load_sem.at[0]),
        pltpu.make_async_copy(weight_hbm, weight, load_sem.at[1]),
        pltpu.make_async_copy(cotangent_hbm, cotangent, load_sem.at[2]),
    ]
    tile_load = pltpu.make_async_copy(tiles_hbm, tiles, tile_sem)
    table_loads = [
        pltpu.make_async_copy(lists.at[0], table_forward, load_sem.at[3]),
        pltpu.make_async_copy(lists.at[1], table_back, load_sem.at[4]),
    ]

    def prepare():
        for copy in loads:
            copy.start()
        tile_load.start()
        panel[32] = jnp.zeros((SIDE, FEAT), BF)
        grads[64] = jnp.zeros((FEAT, SIDE), BF)
        tile_row, tile_col = coords[0:1], coords[1:2]
        live = jnp.where(
            lax.broadcasted_iota(jnp.int32, (1, SLOTS), 1) < count[0, 0], 1, 0
        )
        lists[0] = pair_list(tile_row, tile_col, live, 64, 32, PAIRS_FORWARD)
        lists[1] = pair_list(tile_col, tile_row, live, 32, 64, PAIRS_BACK)
        for copy in table_loads:
            copy.start()
        yield

    first = prepare()
    gather(
        rows_group, send, features, lambda g: panel.at[pl.ds(g * 4, 4)], lambda g, h: None,
        lambda: next(first, None),
    )
    for copy in loads + table_loads:
        copy.wait()
    tile_load.wait()
    tile_sums(False, table_forward, tiles, panel, sums_forward, PAIRS_FORWARD)

    group = cols_group
    order = (
        group.other_far, group.other_up, group.other_down, group.up,
        group.down, group.far, group.other, group.own,
    )
    pairs = []
    for k, g in enumerate(order):
        for t in range(4):
            given[k, t] = sums_forward[table_forward[3, (g * 2 + 1 - core) * 4 + t]]
        pairs.append(send(given.at[k], theirs.at[k], sibling))
    held = {id(g): k for k, g in enumerate(order)}

    def ready(g):
        k = held[id(g)]
        pairs[k].wait_recv()
        for t in range(4):
            mine = sums_forward[table_forward[3, (g * 2 + core) * 4 + t]]
            theirs[k, t] = (theirs[k, t].astype(F32) + mine.astype(F32)).astype(BF)

    terms = scatter_sum(group, send, ready, lambda g: theirs.at[held[id(g)]], got_forward)
    for t in range(4):
        total = terms[0][t].astype(F32)
        for term in terms[1:]:
            total = total + term[t].astype(F32)
        rows = pl.ds(t * SIDE, SIDE)
        high = total.astype(BF)
        low = (total - high.astype(F32)).astype(BF)
        total_hi[rows] = high
        total_lo[rows] = low
        hidden = jnp.dot(high, weight[...], preferred_element_type=F32) + jnp.dot(
            low, weight[...], preferred_element_type=F32
        )
        sigma = 1.0 / (1.0 + jnp.exp(-hidden))
        output[rows] = (hidden * sigma).astype(BF)
        slope = (cotangent[rows].astype(F32) * sigma * (1.0 + hidden * (1.0 - sigma))).astype(BF)
        own[rows] = slope
        grads[group.own * 8 + core * 4 + t] = lax.dot_general(
            weight[...], slope, (((1,), (1,)), ((), ())), preferred_element_type=F32
        ).astype(BF)

    def spot(g):
        return grads.at[pl.ds((g * 2 + core) * 4, 4)]

    def landed(g, h):
        block = spot(g).at[H[h]]
        shared.append(send(block, block, sibling))

    output_copy = pltpu.make_async_copy(output, output_hbm, load_sem.at[5])

    def weight_sum():
        output_copy.start()
        over = (((0,), (0,)), ((), ()))
        whole[...] = lax.dot_general(
            total_hi[...], own[...], over, preferred_element_type=F32
        ) + lax.dot_general(total_lo[...], own[...], over, preferred_element_type=F32)
        yield from ring_sum(rows_group, send, whole, FEAT // 4, row_got, row_met, row_sum, 0)

    shared = []
    stages = weight_sum()
    landed(group.own, 0)
    landed(group.own, 1)
    gather(group, send, spot(group.own), spot, landed, lambda: next(stages, None))
    for _ in stages:
        pass
    for copy in shared:
        copy.wait_recv()
    tile_sums(True, table_back, tiles, grads, sums_back, PAIRS_BACK)

    def gathered(g):
        for t in range(4):
            back[g * 4 + t] = sums_back[table_back[3, g * 4 + t]]

    stages = pair_then_ring_sum(
        cols_group, send, row_sum, half_got, half, col_got, col_met, weight_grad
    )
    terms = scatter_sum(
        rows_group, send, gathered, lambda g: back.at[pl.ds(g * 4, 4)], got_back, lambda: next(stages, None)
    )
    for t in range(4):
        total = terms[0][t].astype(F32)
        for term in terms[1:]:
            total = total + term[t].astype(F32)
        feature_grad[pl.ds(t * SIDE, SIDE)] = total.T.astype(BF)
    feature_copy = pltpu.make_async_copy(feature_grad, feature_hbm, load_sem.at[6])
    feature_copy.start()
    for _ in stages:
        pass
    send.finish()
    output_copy.wait()
    feature_copy.wait()


def local(features, weight, tiles, tile_coords, tile_counts, cotangent):
    nodes = 4 * SIDE
    blocks = lambda *lead: pltpu.VMEM(lead + (SIDE, FEAT), BF)
    turned = lambda *lead: pltpu.VMEM(lead + (FEAT, SIDE), BF)
    matrix = lambda *shape: pltpu.VMEM(shape + (FEAT,), F32)
    copies = 14 + 8 + 14 + 16 + 14 + 7 + 14 + 9
    return pl.pallas_call(
        layer,
        out_shape=(
            jax.ShapeDtypeStruct((nodes, FEAT), BF),
            jax.ShapeDtypeStruct((nodes, FEAT), BF),
            jax.ShapeDtypeStruct((FEAT, FEAT), F32),
        ),
        in_specs=[ANY, ANY, ANY, VMEM, SMEM, ANY],
        out_specs=(ANY, ANY, VMEM),
        scratch_shapes=[
            pltpu.VMEM((SLOTS, SIDE, SIDE), BF),
            blocks(33),
            turned(65),
            blocks(PAIRS_FORWARD + 1),
            turned(PAIRS_BACK + 1),
            blocks(8, 4),
            blocks(8, 4),
            turned(32),
            blocks(7, 4),
            turned(7, 4),
            pltpu.VMEM((2, 8, PLACES), jnp.int32),
            pltpu.SMEM((8, PLACES), jnp.int32),
            pltpu.SMEM((8, PLACES), jnp.int32),
            pltpu.VMEM((FEAT, FEAT), BF),
            pltpu.VMEM((nodes, FEAT), BF),
            pltpu.VMEM((nodes, FEAT), BF),
            pltpu.VMEM((nodes, FEAT), BF),
            pltpu.VMEM((nodes, FEAT), BF),
            pltpu.VMEM((nodes, FEAT), BF),
            pltpu.VMEM((nodes, FEAT), BF),
            matrix(FEAT),
            matrix(FEAT),
            matrix(3, FEAT // 4),
            matrix(2, FEAT // 4),
            matrix(FEAT // 2),
            matrix(FEAT // 2),
            matrix(3, FEAT // 8),
            matrix(2, FEAT // 8),
            pltpu.SemaphoreType.DMA((copies,)),
            pltpu.SemaphoreType.DMA((copies,)),
            pltpu.SemaphoreType.DMA((7,)),
            pltpu.SemaphoreType.DMA,
        ],
        compiler_params=pltpu.CompilerParams(
            collective_id=0, has_side_effects=True, vmem_limit_bytes=VMEM_BYTES
        ),
        name="layer",
    )(
        features.reshape(4, SIDE, FEAT), weight, tiles[0, 0], tile_coords[0, 0], tile_counts, cotangent,
    )


def solution(mesh):
    placed = (
        P(("col", "row"), None),
        P(),
        P("row", "col", None, None, None),
        P("row", "col", None, None),
        P("row", "col"),
        P(("row", "col"), None),
    )
    return jax.shard_map(
        local,
        mesh=mesh,
        in_specs=placed,
        out_specs=(P(("row", "col"), None), P(("col", "row"), None), P()),
        check_vma=False,
    )
```

```python
import functools

import jax
import jax.numpy as jnp
from jax import lax
from jax.experimental import pallas as pl
from jax.experimental.pallas import tpu as pltpu
from jax.sharding import PartitionSpec as P

MESH = pl.DeviceIdType.MESH
BF = jnp.bfloat16
F32 = jnp.float32
ANY = pl.BlockSpec(memory_space=pl.ANY)
VMEM = pl.BlockSpec(memory_space=pltpu.VMEM)
SMEM = pl.BlockSpec(memory_space=pltpu.SMEM)
VMEM_BYTES = 60 * 2**20
SIDE = 128
FEAT = 256
SLOTS = 384
PAIRS_FORWARD = (SLOTS + 64) // 2
PAIRS_BACK = (SLOTS + 32) // 2
STEPS = 8
PLACES = 512
H = (pl.ds(0, 2), pl.ds(2, 2))


class Group:
    def __init__(self, along):
        row = lax.axis_index("row")
        col = lax.axis_index("col")
        if along == "row":
            place = row
            self.device = lambda g: (g, col)
        else:
            place = lax.div(col, 2)
            core = lax.rem(col, 2)
            self.device = lambda g: (row, g * 2 + core)
            self.sibling = (row, place * 2 + 1 - core)
            self.core = core
        a = lax.div(place, 4)
        b = lax.rem(place, 4)
        up = lax.rem(b + 1, 4)
        down = lax.rem(b + 3, 4)
        far = lax.rem(b + 2, 4)
        self.own = place
        self.up, self.down, self.far = a * 4 + up, a * 4 + down, a * 4 + far
        self.other = (1 - a) * 4 + b
        self.other_up, self.other_down, self.other_far = (
            (1 - a) * 4 + up,
            (1 - a) * 4 + down,
            (1 - a) * 4 + far,
        )

    def peers(self):
        return [self.device(g) for g in (self.up, self.down, self.far, self.other)]


def greet(peers):
    barrier = pltpu.get_barrier_semaphore()
    for peer in peers:
        pl.semaphore_signal(barrier, inc=1, device_id=peer, device_id_type=MESH)
    pl.semaphore_wait(barrier, len(peers))


def ring_sum(group, send, whole, size, got, met, out, base):
    rows = lambda b: pl.ds(b * size, size)
    ring = [(group.device(g), lax.rem(g, 4)) for g in (group.up, group.down, group.far)]
    mine = lax.rem(group.own, 4)
    copies = [send(whole.at[rows(b)], got.at[k], peer) for k, (peer, b) in enumerate(ring)]
    yield
    for copy in copies:
        copy.wait_recv()
    met[0] = whole[rows(mine)] + got[0] + got[1] + got[2]
    copy = send(met.at[0], met.at[1], group.device(group.other))
    yield
    copy.wait_recv()
    spot = out.at[pl.ds(base + mine * size, size)]
    spot[...] = met[0] + met[1]
    copies = [send(spot, spot, peer) for peer, _ in ring]
    yield
    for copy in copies:
        copy.wait_recv()


def pair_then_ring_sum(group, send, whole, theirs, half, got, met, out):
    size = whole.shape[0] // 2
    mine = pl.ds(group.core * size, size)
    copy = send(whole.at[pl.ds((1 - group.core) * size, size)], theirs, group.sibling)
    yield
    copy.wait_recv()
    half[...] = whole[mine] + theirs[...]
    yield from ring_sum(group, send, half, size // 4, got, met, out, group.core * size)
    copy = send(out.at[mine], out.at[mine], group.sibling)
    yield
    copy.wait_recv()


class Sender:
    def __init__(self, send_sem, recv_sem):
        self.send_sem, self.recv_sem = send_sem, recv_sem
        self.used = 0
        self.all = []

    def __call__(self, src, dst, device):
        copy = pltpu.make_async_remote_copy(
            src_ref=src,
            dst_ref=dst,
            send_sem=self.send_sem.at[self.used],
            recv_sem=self.recv_sem.at[self.used],
            device_id=device,
            device_id_type=MESH,
        )
        self.used += 1
        self.all.append(copy)
        copy.start()
        return copy

    def finish(self):
        for copy in self.all:
            copy.wait_send()


def gather(group, send, own, spot, landed, tick=lambda: None):
    up, down, other = (group.device(g) for g in (group.up, group.down, group.other))
    here = spot(group.own)
    c_up, c_down, c_other = [None, None], [None, None], [None, None]
    for h in (0, 1):
        c_up[h] = send(own.at[H[h]], here.at[H[h]], up)
        c_down[1 - h] = send(own.at[H[1 - h]], here.at[H[1 - h]], down)
        c_other[h] = send(own.at[H[h]], here.at[H[h]], other)
    tick()
    f_up, f_down = [None, None], [None, None]
    c_up[0].wait_recv()
    far_first = send(spot(group.down).at[H[0]], spot(group.down).at[H[0]], up)
    landed(group.down, 0)
    c_down[1].wait_recv()
    far_second = send(spot(group.up).at[H[1]], spot(group.up).at[H[1]], down)
    landed(group.up, 1)
    for h in (0, 1):
        c_other[h].wait_recv()
        block = spot(group.other).at[H[h]]
        f_up[h] = send(block, block, up)
        f_down[h] = send(block, block, down)
        landed(group.other, h)
    tick()
    c_up[1].wait_recv()
    landed(group.down, 1)
    c_down[0].wait_recv()
    landed(group.up, 0)
    far_first.wait_recv()
    block = spot(group.far).at[H[0]]
    x_first = send(block, block, other)
    landed(group.far, 0)
    far_second.wait_recv()
    block = spot(group.far).at[H[1]]
    x_second = send(block, block, other)
    landed(group.far, 1)
    tick()
    for h in (0, 1):
        f_up[h].wait_recv()
        landed(group.other_down, h)
        f_down[h].wait_recv()
        landed(group.other_up, h)
    x_first.wait_recv()
    landed(group.other_far, 0)
    x_second.wait_recv()
    landed(group.other_far, 1)


def plus(target, *terms):
    total = terms[0][...].astype(F32)
    for term in terms[1:]:
        total = total + term[...].astype(F32)
    target[...] = total.astype(target.dtype)


def scatter_sum(group, send, ready, spot, got, tick=lambda: None):
    r1, r2d, r2u, r3, r4d, r4u, r5 = (got.at[k] for k in range(7))
    up, down, other = (group.device(g) for g in (group.up, group.down, group.other))
    ready(group.other_far)
    c1 = [send(spot(group.other_far).at[H[h]], r1.at[H[h]], other) for h in (0, 1)]
    ready(group.other_up)
    c2u = [send(spot(group.other_up).at[H[h]], r2d.at[H[h]], up) for h in (0, 1)]
    ready(group.other_down)
    c2d = [send(spot(group.other_down).at[H[h]], r2u.at[H[h]], down) for h in (0, 1)]
    ready(group.up)
    c4u, c4d = [None, None], [None, None]
    c4u[1] = send(spot(group.up).at[H[1]], r4d.at[H[1]], up)
    ready(group.down)
    c4d[0] = send(spot(group.down).at[H[0]], r4u.at[H[0]], down)
    ready(group.far)
    tick()
    c1[0].wait_recv()
    plus(r1.at[H[0]], r1.at[H[0]], spot(group.far).at[H[0]])
    c3u = send(r1.at[H[0]], r3.at[H[0]], up)
    tick()
    c1[1].wait_recv()
    plus(r1.at[H[1]], r1.at[H[1]], spot(group.far).at[H[1]])
    c3d = send(r1.at[H[1]], r3.at[H[1]], down)
    ready(group.other)
    tick()
    c5 = []
    for h in (0, 1):
        c2u[h].wait_recv()
        c2d[h].wait_recv()
        plus(r2d.at[H[h]], r2d.at[H[h]], r2u.at[H[h]], spot(group.other).at[H[h]])
        c5.append(send(r2d.at[H[h]], r5.at[H[h]], other))
        tick()
    c3u.wait_recv()
    plus(r3.at[H[0]], r3.at[H[0]], spot(group.up).at[H[0]])
    c4u[0] = send(r3.at[H[0]], r4d.at[H[0]], up)
    c3d.wait_recv()
    plus(r3.at[H[1]], r3.at[H[1]], spot(group.down).at[H[1]])
    c4d[1] = send(r3.at[H[1]], r4u.at[H[1]], down)
    ready(group.own)
    for copies in (c5, c4u, c4d):
        for copy in copies:
            copy.wait_recv()
    return (spot(group.own), r4d, r4u, r5)


def pair_list(key, source, live, outs, empty, pairs):
    def iota(shape, dim):
        return lax.broadcasted_iota(jnp.int32, shape, dim)

    def add(x, axis):
        return jnp.sum(x, axis=axis, keepdims=True, dtype=jnp.int32)

    def upright(x):
        n = x.shape[1]
        return add(jnp.where(iota((n, n), 0) == iota((n, n), 1), x, 0), 1)

    key_up, source_up, live_up = upright(key), upright(source), upright(live)
    square = (SLOTS, SLOTS)
    before = (key_up == key) & (iota(square, 1) < iota(square, 0))
    rank = add(jnp.where(before, live, 0), 1)
    member = jnp.where(key_up == iota((SLOTS, SIDE), 1), live_up, 0)
    held = (add(member, 0) + 1) >> 1
    tri = (SIDE, SIDE)
    start = add(jnp.where(iota(tri, 0) < iota(tri, 1), upright(held), 0), 0)
    place = jnp.where(live_up > 0, 2 * add(member * start, 1) + rank, -1)
    wide = (SLOTS, PLACES)
    hit = place == iota(wide, 1)
    slots = add(jnp.where(hit, iota(wide, 0), 0), 0)
    sources = add(jnp.where(hit, source_up - empty, 0), 0) + empty
    firsts = add(jnp.where(hit & (rank == 0), 1, 0), 0)
    last = jnp.where(held > 0, start + held - 1, pairs)
    last = jnp.concatenate([last, jnp.zeros((1, PLACES - SIDE), jnp.int32)], axis=1)
    row = iota((8, PLACES), 0)
    return jnp.where(row == 0, slots, jnp.where(row == 1, sources, jnp.where(row == 2, firsts, last)))


def tile_sums(transpose, table, tiles, panel, sums, pairs):
    block = sums.shape[1:]
    sums[pairs] = jnp.zeros(block, BF)

    unroll = pairs // STEPS

    def several(i, run):
        for u in range(unroll):
            q = i * unroll + u
            values = [tiles[table[0, 2 * q + k]] for k in (0, 1)]
            sources = [panel[table[1, 2 * q + k]] for k in (0, 1)]
            left, right = jnp.concatenate(values, 0 if transpose else 1), jnp.concatenate(sources, 0)
            run = jnp.where(table[2, 2 * q] == 1, 0.0, run)
            run = run + lax.dot_general(
                left, right, (((0 if transpose else 1,), (0,)), ((), ())), preferred_element_type=F32
            )
            sums[q] = run.astype(BF)
        return run

    lax.fori_loop(0, STEPS, several, jnp.zeros(block, F32))


def layer(
    features, weight_hbm, tiles_hbm, coords, count, cotangent_hbm,
    output_hbm, feature_hbm, weight_grad_hbm,
    tiles, panel, grads, sums_forward, sums_back, given, theirs, back, got_forward, got_back,
    lists, table_forward, table_back, weight, cotangent, output, feature_grad, weight_grad,
    total_hi, total_lo, own, whole, row_sum, row_got, row_met, half, half_got, col_got, col_met,
    send_sem, recv_sem, load_sem, tile_sem,
):
    rows_group, cols_group = Group("row"), Group("col")
    core, sibling = cols_group.core, cols_group.sibling
    greet(rows_group.peers() + cols_group.peers() + [sibling])
    send = Sender(send_sem, recv_sem)
    loads = [
        pltpu.make_async_copy(features, panel.at[pl.ds(rows_group.own * 4, 4)], load_sem.at[0]),
        pltpu.make_async_copy(weight_hbm, weight, load_sem.at[1]),
        pltpu.make_async_copy(cotangent_hbm, cotangent, load_sem.at[2]),
    ]
    tile_load = pltpu.make_async_copy(tiles_hbm, tiles, tile_sem)
    table_loads = [
        pltpu.make_async_copy(lists.at[0], table_forward, load_sem.at[3]),
        pltpu.make_async_copy(lists.at[1], table_back, load_sem.at[4]),
    ]

    def prepare():
        for copy in loads:
            copy.start()
        tile_load.start()
        panel[32] = jnp.zeros((SIDE, FEAT), BF)
        grads[64] = jnp.zeros((SIDE, FEAT), BF)
        tile_row, tile_col = coords[0:1], coords[1:2]
        live = jnp.where(
            lax.broadcasted_iota(jnp.int32, (1, SLOTS), 1) < count[0, 0], 1, 0
        )
        lists[0] = pair_list(tile_row, tile_col, live, 64, 32, PAIRS_FORWARD)
        lists[1] = pair_list(tile_col, tile_row, live, 32, 64, PAIRS_BACK)
        for copy in table_loads:
            copy.start()
        yield

    first = prepare()
    gather(
        rows_group, send, features, lambda g: panel.at[pl.ds(g * 4, 4)], lambda g, h: None,
        lambda: next(first, None),
    )
    for copy in loads + table_loads:
        copy.wait()
    tile_load.wait()
    tile_sums(False, table_forward, tiles, panel, sums_forward, PAIRS_FORWARD)

    group = cols_group
    order = (
        group.other_far, group.other_up, group.other_down, group.up,
        group.down, group.far, group.other, group.own,
    )
    pairs = []
    for k, g in enumerate(order):
        for t in range(4):
            given[k, t] = sums_forward[table_forward[3, (g * 2 + 1 - core) * 4 + t]]
        pairs.append(send(given.at[k], theirs.at[k], sibling))
    held = {id(g): k for k, g in enumerate(order)}

    def ready(g):
        k = held[id(g)]
        pairs[k].wait_recv()
        for t in range(4):
            mine = sums_forward[table_forward[3, (g * 2 + core) * 4 + t]]
            theirs[k, t] = (theirs[k, t].astype(F32) + mine.astype(F32)).astype(BF)

    terms = scatter_sum(group, send, ready, lambda g: theirs.at[held[id(g)]], got_forward)
    for t in range(4):
        total = terms[0][t].astype(F32)
        for term in terms[1:]:
            total = total + term[t].astype(F32)
        rows = pl.ds(t * SIDE, SIDE)
        high = total.astype(BF)
        low = (total - high.astype(F32)).astype(BF)
        total_hi[rows] = high
        total_lo[rows] = low
        hidden = jnp.dot(high, weight[...], preferred_element_type=F32) + jnp.dot(
            low, weight[...], preferred_element_type=F32
        )
        sigma = 1.0 / (1.0 + jnp.exp(-hidden))
        output[rows] = (hidden * sigma).astype(BF)
        slope = (cotangent[rows].astype(F32) * sigma * (1.0 + hidden * (1.0 - sigma))).astype(BF)
        own[rows] = slope
        grads[group.own * 8 + core * 4 + t] = lax.dot_general(
            slope, weight[...], (((1,), (1,)), ((), ())), preferred_element_type=F32
        ).astype(BF)

    def spot(g):
        return grads.at[pl.ds((g * 2 + core) * 4, 4)]

    def landed(g, h):
        block = spot(g).at[H[h]]
        shared.append(send(block, block, sibling))

    output_copy = pltpu.make_async_copy(output, output_hbm, load_sem.at[5])

    def weight_sum():
        output_copy.start()
        over = (((0,), (0,)), ((), ()))
        whole[...] = lax.dot_general(
            total_hi[...], own[...], over, preferred_element_type=F32
        ) + lax.dot_general(total_lo[...], own[...], over, preferred_element_type=F32)
        yield from ring_sum(rows_group, send, whole, FEAT // 4, row_got, row_met, row_sum, 0)

    shared = []
    stages = weight_sum()
    landed(group.own, 0)
    landed(group.own, 1)
    gather(group, send, spot(group.own), spot, landed, lambda: next(stages, None))
    for _ in stages:
        pass
    for copy in shared:
        copy.wait_recv()
    tile_sums(True, table_back, tiles, grads, sums_back, PAIRS_BACK)

    def gathered(g):
        for t in range(4):
            back[g * 4 + t] = sums_back[table_back[3, g * 4 + t]]

    stages = pair_then_ring_sum(
        cols_group, send, row_sum, half_got, half, col_got, col_met, weight_grad
    )
    terms = scatter_sum(
        rows_group, send, gathered, lambda g: back.at[pl.ds(g * 4, 4)], got_back, lambda: next(stages, None)
    )
    for t in range(4):
        total = terms[0][t].astype(F32)
        for term in terms[1:]:
            total = total + term[t].astype(F32)
        feature_grad[pl.ds(t * SIDE, SIDE)] = total.astype(BF)
    feature_copy = pltpu.make_async_copy(feature_grad, feature_hbm, load_sem.at[6])
    feature_copy.start()
    for _ in stages:
        pass
    weight_copy = pltpu.make_async_copy(weight_grad, weight_grad_hbm, load_sem.at[7])
    weight_copy.start()
    send.finish()
    output_copy.wait()
    feature_copy.wait()
    weight_copy.wait()


def deliver(*refs):
    count = len(refs) // 2
    for k in range(count):
        refs[count + k][...] = refs[k][...]


def local(features, weight, tiles, tile_coords, tile_counts, cotangent):
    nodes = 4 * SIDE
    blocks = lambda *lead: pltpu.VMEM(lead + (SIDE, FEAT), BF)
    matrix = lambda *shape: pltpu.VMEM(shape + (FEAT,), F32)
    copies = 14 + 8 + 14 + 16 + 14 + 7 + 14 + 9
    shapes = (
        jax.ShapeDtypeStruct((nodes, FEAT), BF),
        jax.ShapeDtypeStruct((nodes, FEAT), BF),
        jax.ShapeDtypeStruct((FEAT, FEAT), F32),
    )
    results = pl.pallas_call(
        layer,
        out_shape=shapes,
        in_specs=[ANY, ANY, ANY, VMEM, SMEM, ANY],
        out_specs=(ANY, ANY, ANY),
        scratch_shapes=[
            pltpu.VMEM((SLOTS, SIDE, SIDE), BF),
            blocks(33),
            blocks(65),
            blocks(PAIRS_FORWARD + 1),
            blocks(PAIRS_BACK + 1),
            blocks(8, 4),
            blocks(8, 4),
            blocks(32),
            blocks(7, 4),
            blocks(7, 4),
            pltpu.VMEM((2, 8, PLACES), jnp.int32),
            pltpu.SMEM((8, PLACES), jnp.int32),
            pltpu.SMEM((8, PLACES), jnp.int32),
            pltpu.VMEM((FEAT, FEAT), BF),
            pltpu.VMEM((nodes, FEAT), BF),
            pltpu.VMEM((nodes, FEAT), BF),
            pltpu.VMEM((nodes, FEAT), BF),
            matrix(FEAT),
            pltpu.VMEM((nodes, FEAT), BF),
            pltpu.VMEM((nodes, FEAT), BF),
            pltpu.VMEM((nodes, FEAT), BF),
            matrix(FEAT),
            matrix(FEAT),
            matrix(3, FEAT // 4),
            matrix(2, FEAT // 4),
            matrix(FEAT // 2),
            matrix(FEAT // 2),
            matrix(3, FEAT // 8),
            matrix(2, FEAT // 8),
            pltpu.SemaphoreType.DMA((copies,)),
            pltpu.SemaphoreType.DMA((copies,)),
            pltpu.SemaphoreType.DMA((8,)),
            pltpu.SemaphoreType.DMA,
        ],
        compiler_params=pltpu.CompilerParams(
            collective_id=0, has_side_effects=True, vmem_limit_bytes=VMEM_BYTES
        ),
        name="layer",
    )(
        features.reshape(4, SIDE, FEAT), weight, tiles[0, 0], tile_coords[0, 0], tile_counts, cotangent,
    )
    return pl.pallas_call(
        deliver,
        out_shape=shapes,
        in_specs=[VMEM, VMEM, VMEM],
        out_specs=(VMEM, VMEM, VMEM),
        name="deliver",
    )(*results)


def solution(mesh):
    placed = (
        P(("col", "row"), None),
        P(),
        P("row", "col", None, None, None),
        P("row", "col", None, None),
        P("row", "col"),
        P(("row", "col"), None),
    )
    return jax.shard_map(
        local,
        mesh=mesh,
        in_specs=placed,
        out_specs=(P(("row", "col"), None), P(("col", "row"), None), P()),
        check_vma=False,
    )
```

```python
import functools

import jax
import jax.numpy as jnp
from jax import lax
from jax.experimental import pallas as pl
from jax.experimental.pallas import tpu as pltpu
from jax.sharding import PartitionSpec as P

MESH = pl.DeviceIdType.MESH
BF = jnp.bfloat16
F32 = jnp.float32
ANY = pl.BlockSpec(memory_space=pl.ANY)
VMEM = pl.BlockSpec(memory_space=pltpu.VMEM)
SMEM = pl.BlockSpec(memory_space=pltpu.SMEM)
VMEM_BYTES = 60 * 2**20
SIDE = 128
FEAT = 256
SLOTS = 384
PAIRS_FORWARD = (SLOTS + 64) // 2
PAIRS_BACK = (SLOTS + 32) // 2
CUTS = (0, 66, 132, 198, PAIRS_FORWARD)
STEPS = 2
PLACES = 512
H = (pl.ds(0, 2), pl.ds(2, 2))


class Group:
    def __init__(self, along):
        row = lax.axis_index("row")
        col = lax.axis_index("col")
        if along == "row":
            place = row
            self.device = lambda g: (g, col)
        else:
            place = lax.div(col, 2)
            core = lax.rem(col, 2)
            self.device = lambda g: (row, g * 2 + core)
            self.sibling = (row, place * 2 + 1 - core)
            self.core = core
        a = lax.div(place, 4)
        b = lax.rem(place, 4)
        up = lax.rem(b + 1, 4)
        down = lax.rem(b + 3, 4)
        far = lax.rem(b + 2, 4)
        self.own = place
        self.up, self.down, self.far = a * 4 + up, a * 4 + down, a * 4 + far
        self.other = (1 - a) * 4 + b
        self.other_up, self.other_down, self.other_far = (
            (1 - a) * 4 + up,
            (1 - a) * 4 + down,
            (1 - a) * 4 + far,
        )

    def peers(self):
        return [self.device(g) for g in (self.up, self.down, self.far, self.other)]


def greet(peers):
    barrier = pltpu.get_barrier_semaphore()
    for peer in peers:
        pl.semaphore_signal(barrier, inc=1, device_id=peer, device_id_type=MESH)
    pl.semaphore_wait(barrier, len(peers))


def ring_sum(group, send, whole, size, got, met, out, base):
    rows = lambda b: pl.ds(b * size, size)
    ring = [(group.device(g), lax.rem(g, 4)) for g in (group.up, group.down, group.far)]
    mine = lax.rem(group.own, 4)
    copies = [send(whole.at[rows(b)], got.at[k], peer) for k, (peer, b) in enumerate(ring)]
    yield
    for copy in copies:
        copy.wait_recv()
    met[0] = whole[rows(mine)] + got[0] + got[1] + got[2]
    copy = send(met.at[0], met.at[1], group.device(group.other))
    yield
    copy.wait_recv()
    spot = out.at[pl.ds(base + mine * size, size)]
    spot[...] = met[0] + met[1]
    copies = [send(spot, spot, peer) for peer, _ in ring]
    yield
    for copy in copies:
        copy.wait_recv()


def pair_then_ring_sum(group, send, whole, theirs, half, got, met, out):
    size = whole.shape[0] // 2
    mine = pl.ds(group.core * size, size)
    copy = send(whole.at[pl.ds((1 - group.core) * size, size)], theirs, group.sibling)
    yield
    copy.wait_recv()
    half[...] = whole[mine] + theirs[...]
    yield from ring_sum(group, send, half, size // 4, got, met, out, group.core * size)
    copy = send(out.at[mine], out.at[mine], group.sibling)
    yield
    copy.wait_recv()


def in_turn(tile_row):
    col = lax.axis_index("col")
    core, b, a = lax.rem(col, 2), lax.rem(lax.div(col, 2), 4), lax.div(col, 8)
    side = jnp.where((tile_row >> 5) == a, 4, 0)
    kin = jnp.where(((tile_row >> 2) & 1) == core, 8, 0)
    steps = (((tile_row >> 3) & 3) + 4 - b) & 3
    place = jnp.where(steps == 0, 3, jnp.where(steps == 1, 0, jnp.where(steps == 2, 2, 1)))
    return (kin + side + place) * 4 + (tile_row & 3)


class Sender:
    def __init__(self, send_sem, recv_sem):
        self.send_sem, self.recv_sem = send_sem, recv_sem
        self.used = 0
        self.all = []

    def __call__(self, src, dst, device):
        copy = pltpu.make_async_remote_copy(
            src_ref=src,
            dst_ref=dst,
            send_sem=self.send_sem.at[self.used],
            recv_sem=self.recv_sem.at[self.used],
            device_id=device,
            device_id_type=MESH,
        )
        self.used += 1
        self.all.append(copy)
        copy.start()
        return copy

    def finish(self):
        for copy in self.all:
            copy.wait_send()


def gather(group, send, own, spot, landed, tick=lambda: None):
    up, down, other = (group.device(g) for g in (group.up, group.down, group.other))
    here = spot(group.own)
    c_up, c_down, c_other = [None, None], [None, None], [None, None]
    for h in (0, 1):
        c_up[h] = send(own.at[H[h]], here.at[H[h]], up)
        c_down[1 - h] = send(own.at[H[1 - h]], here.at[H[1 - h]], down)
        c_other[h] = send(own.at[H[h]], here.at[H[h]], other)
    tick()
    f_up, f_down = [None, None], [None, None]
    c_up[0].wait_recv()
    far_first = send(spot(group.down).at[H[0]], spot(group.down).at[H[0]], up)
    landed(group.down, 0)
    c_down[1].wait_recv()
    far_second = send(spot(group.up).at[H[1]], spot(group.up).at[H[1]], down)
    landed(group.up, 1)
    for h in (0, 1):
        c_other[h].wait_recv()
        block = spot(group.other).at[H[h]]
        f_up[h] = send(block, block, up)
        f_down[h] = send(block, block, down)
        landed(group.other, h)
    tick()
    c_up[1].wait_recv()
    landed(group.down, 1)
    c_down[0].wait_recv()
    landed(group.up, 0)
    far_first.wait_recv()
    block = spot(group.far).at[H[0]]
    x_first = send(block, block, other)
    landed(group.far, 0)
    far_second.wait_recv()
    block = spot(group.far).at[H[1]]
    x_second = send(block, block, other)
    landed(group.far, 1)
    tick()
    for h in (0, 1):
        f_up[h].wait_recv()
        landed(group.other_down, h)
        f_down[h].wait_recv()
        landed(group.other_up, h)
    x_first.wait_recv()
    landed(group.other_far, 0)
    x_second.wait_recv()
    landed(group.other_far, 1)


def plus(target, *terms):
    total = terms[0][...].astype(F32)
    for term in terms[1:]:
        total = total + term[...].astype(F32)
    target[...] = total.astype(target.dtype)


def scatter_sum(group, send, ready, spot, got, tick=lambda: None):
    r1, r2d, r2u, r3, r4d, r4u, r5 = (got.at[k] for k in range(7))
    up, down, other = (group.device(g) for g in (group.up, group.down, group.other))
    ready(group.other_up)
    c2u = [send(spot(group.other_up).at[H[h]], r2d.at[H[h]], up) for h in (0, 1)]
    ready(group.other_down)
    c2d = [send(spot(group.other_down).at[H[h]], r2u.at[H[h]], down) for h in (0, 1)]
    ready(group.other_far)
    c1 = [send(spot(group.other_far).at[H[h]], r1.at[H[h]], other) for h in (0, 1)]
    ready(group.up)
    c4u, c4d = [None, None], [None, None]
    c4u[1] = send(spot(group.up).at[H[1]], r4d.at[H[1]], up)
    ready(group.down)
    c4d[0] = send(spot(group.down).at[H[0]], r4u.at[H[0]], down)
    ready(group.far)
    tick()
    c1[0].wait_recv()
    plus(r1.at[H[0]], r1.at[H[0]], spot(group.far).at[H[0]])
    c3u = send(r1.at[H[0]], r3.at[H[0]], up)
    tick()
    c1[1].wait_recv()
    plus(r1.at[H[1]], r1.at[H[1]], spot(group.far).at[H[1]])
    c3d = send(r1.at[H[1]], r3.at[H[1]], down)
    ready(group.other)
    tick()
    c5 = []
    for h in (0, 1):
        c2u[h].wait_recv()
        c2d[h].wait_recv()
        plus(r2d.at[H[h]], r2d.at[H[h]], r2u.at[H[h]], spot(group.other).at[H[h]])
        c5.append(send(r2d.at[H[h]], r5.at[H[h]], other))
        tick()
    c3u.wait_recv()
    plus(r3.at[H[0]], r3.at[H[0]], spot(group.up).at[H[0]])
    c4u[0] = send(r3.at[H[0]], r4d.at[H[0]], up)
    c3d.wait_recv()
    plus(r3.at[H[1]], r3.at[H[1]], spot(group.down).at[H[1]])
    c4d[1] = send(r3.at[H[1]], r4u.at[H[1]], down)
    ready(group.own)
    for copies in (c5, c4u, c4d):
        for copy in copies:
            copy.wait_recv()
    return (spot(group.own), r4d, r4u, r5)


def pair_list(key, source, live, outs, empty, pairs):
    def iota(shape, dim):
        return lax.broadcasted_iota(jnp.int32, shape, dim)

    def add(x, axis):
        return jnp.sum(x, axis=axis, keepdims=True, dtype=jnp.int32)

    def upright(x):
        n = x.shape[1]
        return add(jnp.where(iota((n, n), 0) == iota((n, n), 1), x, 0), 1)

    key_up, source_up, live_up = upright(key), upright(source), upright(live)
    square = (SLOTS, SLOTS)
    before = (key_up == key) & (iota(square, 1) < iota(square, 0))
    rank = add(jnp.where(before, live, 0), 1)
    member = jnp.where(key_up == iota((SLOTS, SIDE), 1), live_up, 0)
    held = (add(member, 0) + 1) >> 1
    tri = (SIDE, SIDE)
    start = add(jnp.where(iota(tri, 0) < iota(tri, 1), upright(held), 0), 0)
    place = jnp.where(live_up > 0, 2 * add(member * start, 1) + rank, -1)
    wide = (SLOTS, PLACES)
    hit = place == iota(wide, 1)
    slots = add(jnp.where(hit, iota(wide, 0), 0), 0)
    sources = add(jnp.where(hit, source_up - empty, 0), 0) + empty
    firsts = add(jnp.where(hit & (rank == 0), 1, 0), 0)
    last = jnp.where(held > 0, start + held - 1, pairs)
    last = jnp.concatenate([last, jnp.zeros((1, PLACES - SIDE), jnp.int32)], axis=1)
    row = iota((8, PLACES), 0)
    return jnp.where(row == 0, slots, jnp.where(row == 1, sources, jnp.where(row == 2, firsts, last)))


def tile_step(transpose, table, tiles, panel, sums, q, run):
    values = [tiles[table[0, 2 * q + k]] for k in (0, 1)]
    sources = [panel[table[1, 2 * q + k]] for k in (0, 1)]
    left, right = jnp.concatenate(values, 0 if transpose else 1), jnp.concatenate(sources, 0)
    run = jnp.where(table[2, 2 * q] == 1, 0.0, run)
    run = run + lax.dot_general(
        left, right, (((0 if transpose else 1,), (0,)), ((), ())), preferred_element_type=F32
    )
    sums[q] = run.astype(BF)
    return run


def tile_sums(transpose, table, tiles, panel, sums, first, last, run, steps):
    unroll = (last - first) // steps

    def several(i, run):
        for u in range(unroll):
            run = tile_step(transpose, table, tiles, panel, sums, first + i * unroll + u, run)
        return run

    return lax.fori_loop(0, steps, several, run)


def layer(
    features, weight_hbm, tiles_hbm, coords, count, cotangent_hbm,
    output_hbm, feature_hbm, weight_grad_hbm,
    tiles, panel, grads, sums_forward, sums_back, given, theirs, back, got_forward, got_back,
    lists, table_forward, table_back, weight, cotangent, output, feature_grad, weight_grad,
    total_hi, total_lo, own, whole, row_sum, row_got, row_met, half, half_got, col_got, col_met,
    send_sem, recv_sem, load_sem, tile_sem,
):
    rows_group, cols_group = Group("row"), Group("col")
    core, sibling = cols_group.core, cols_group.sibling
    greet(rows_group.peers() + cols_group.peers() + [sibling])
    send = Sender(send_sem, recv_sem)
    loads = [
        pltpu.make_async_copy(features, panel.at[pl.ds(rows_group.own * 4, 4)], load_sem.at[0]),
        pltpu.make_async_copy(weight_hbm, weight, load_sem.at[1]),
        pltpu.make_async_copy(cotangent_hbm, cotangent, load_sem.at[2]),
    ]
    tile_load = pltpu.make_async_copy(tiles_hbm, tiles, tile_sem)
    table_loads = [
        pltpu.make_async_copy(lists.at[0], table_forward, load_sem.at[3]),
        pltpu.make_async_copy(lists.at[1], table_back, load_sem.at[4]),
    ]

    def prepare():
        for copy in loads:
            copy.start()
        tile_load.start()
        panel[32] = jnp.zeros((SIDE, FEAT), BF)
        grads[64] = jnp.zeros((SIDE, FEAT), BF)
        tile_row, tile_col = coords[0:1], coords[1:2]
        live = jnp.where(
            lax.broadcasted_iota(jnp.int32, (1, SLOTS), 1) < count[0, 0], 1, 0
        )
        lists[0] = pair_list(in_turn(tile_row), tile_col, live, 64, 32, PAIRS_FORWARD)
        lists[1] = pair_list(tile_col, tile_row, live, 32, 64, PAIRS_BACK)
        for copy in table_loads:
            copy.start()
        yield

    first = prepare()
    gather(
        rows_group, send, features, lambda g: panel.at[pl.ds(g * 4, 4)], lambda g, h: None,
        lambda: next(first, None),
    )
    for copy in loads + table_loads:
        copy.wait()
    tile_load.wait()
    group = cols_group
    order = (
        group.other_up, group.other_down, group.other_far, group.other,
        group.up, group.down, group.far, group.own,
    )
    held = {id(g): k for k, g in enumerate(order)}
    pairs = []

    def give(k):
        for t in range(4):
            given[k, t] = sums_forward[table_forward[3, k * 4 + t]]
        pairs.append(send(given.at[k], theirs.at[k], sibling))

    block = (SIDE, FEAT)
    sums_forward[PAIRS_FORWARD] = jnp.zeros(block, BF)
    run = jnp.zeros(block, F32)
    for k, (begin, end) in enumerate(zip(CUTS[:-1], CUTS[1:])):
        run = tile_sums(
            False, table_forward, tiles, panel, sums_forward, begin, end, run, 2
        )
        if k < 3:
            give(k)
    for k in range(3, 8):
        give(k)

    def ready(g):
        k = held[id(g)]
        pairs[k].wait_recv()
        for t in range(4):
            mine = sums_forward[table_forward[3, (k + 8) * 4 + t]]
            theirs[k, t] = (theirs[k, t].astype(F32) + mine.astype(F32)).astype(BF)

    terms = scatter_sum(group, send, ready, lambda g: theirs.at[held[id(g)]], got_forward)
    for t in range(4):
        total = terms[0][t].astype(F32)
        for term in terms[1:]:
            total = total + term[t].astype(F32)
        rows = pl.ds(t * SIDE, SIDE)
        high = total.astype(BF)
        low = (total - high.astype(F32)).astype(BF)
        total_hi[rows] = high
        total_lo[rows] = low
        hidden = jnp.dot(high, weight[...], preferred_element_type=F32) + jnp.dot(
            low, weight[...], preferred_element_type=F32
        )
        sigma = 1.0 / (1.0 + jnp.exp(-hidden))
        output[rows] = (hidden * sigma).astype(BF)
        slope = (cotangent[rows].astype(F32) * sigma * (1.0 + hidden * (1.0 - sigma))).astype(BF)
        own[rows] = slope
        grads[group.own * 8 + core * 4 + t] = lax.dot_general(
            slope, weight[...], (((1,), (1,)), ((), ())), preferred_element_type=F32
        ).astype(BF)

    def spot(g):
        return grads.at[pl.ds((g * 2 + core) * 4, 4)]

    def landed(g, h):
        block = spot(g).at[H[h]]
        shared.append(send(block, block, sibling))

    output_copy = pltpu.make_async_copy(output, output_hbm, load_sem.at[5])

    def weight_sum():
        output_copy.start()
        over = (((0,), (0,)), ((), ()))
        whole[...] = lax.dot_general(
            total_hi[...], own[...], over, preferred_element_type=F32
        ) + lax.dot_general(total_lo[...], own[...], over, preferred_element_type=F32)
        yield from ring_sum(rows_group, send, whole, FEAT // 4, row_got, row_met, row_sum, 0)

    shared = []
    stages = weight_sum()
    landed(group.own, 0)
    landed(group.own, 1)
    gather(group, send, spot(group.own), spot, landed, lambda: next(stages, None))
    for _ in stages:
        pass
    for copy in shared:
        copy.wait_recv()
    sums_back[PAIRS_BACK] = jnp.zeros(block, BF)
    tile_sums(
        True, table_back, tiles, grads, sums_back, 0, PAIRS_BACK, jnp.zeros(block, F32), STEPS
    )

    def gathered(g):
        for t in range(4):
            back[g * 4 + t] = sums_back[table_back[3, g * 4 + t]]

    stages = pair_then_ring_sum(
        cols_group, send, row_sum, half_got, half, col_got, col_met, weight_grad
    )
    terms = scatter_sum(
        rows_group, send, gathered, lambda g: back.at[pl.ds(g * 4, 4)], got_back, lambda: next(stages, None)
    )
    for t in range(4):
        total = terms[0][t].astype(F32)
        for term in terms[1:]:
            total = total + term[t].astype(F32)
        feature_grad[pl.ds(t * SIDE, SIDE)] = total.astype(BF)
    feature_copy = pltpu.make_async_copy(feature_grad, feature_hbm, load_sem.at[6])
    feature_copy.start()
    for _ in stages:
        pass
    weight_copy = pltpu.make_async_copy(weight_grad, weight_grad_hbm, load_sem.at[7])
    weight_copy.start()
    send.finish()
    output_copy.wait()
    feature_copy.wait()
    weight_copy.wait()


def deliver(*refs):
    count = (len(refs) - 2) // 3
    into, out = refs[-2], refs[-1]
    sources, targets, held = refs[:count], refs[count : 2 * count], refs[2 * count : 3 * count]
    first = [pltpu.make_async_copy(sources[k], held[k], into.at[k]) for k in range(count)]
    second = [pltpu.make_async_copy(held[k], targets[k], out.at[k]) for k in range(count)]
    for copy in first:
        copy.start()
    for k in range(count):
        first[k].wait()
        second[k].start()
    for copy in second:
        copy.wait()


def local(features, weight, tiles, tile_coords, tile_counts, cotangent):
    nodes = 4 * SIDE
    blocks = lambda *lead: pltpu.VMEM(lead + (SIDE, FEAT), BF)
    matrix = lambda *shape: pltpu.VMEM(shape + (FEAT,), F32)
    copies = 14 + 8 + 14 + 16 + 14 + 7 + 14 + 9
    shapes = (
        jax.ShapeDtypeStruct((nodes, FEAT), BF),
        jax.ShapeDtypeStruct((nodes, FEAT), BF),
        jax.ShapeDtypeStruct((FEAT, FEAT), F32),
    )
    results = pl.pallas_call(
        layer,
        out_shape=shapes,
        in_specs=[ANY, ANY, ANY, VMEM, SMEM, ANY],
        out_specs=(ANY, ANY, ANY),
        scratch_shapes=[
            pltpu.VMEM((SLOTS, SIDE, SIDE), BF),
            blocks(33),
            blocks(65),
            blocks(PAIRS_FORWARD + 1),
            blocks(PAIRS_BACK + 1),
            blocks(8, 4),
            blocks(8, 4),
            blocks(32),
            blocks(7, 4),
            blocks(7, 4),
            pltpu.VMEM((2, 8, PLACES), jnp.int32),
            pltpu.SMEM((8, PLACES), jnp.int32),
            pltpu.SMEM((8, PLACES), jnp.int32),
            pltpu.VMEM((FEAT, FEAT), BF),
            pltpu.VMEM((nodes, FEAT), BF),
            pltpu.VMEM((nodes, FEAT), BF),
            pltpu.VMEM((nodes, FEAT), BF),
            matrix(FEAT),
            pltpu.VMEM((nodes, FEAT), BF),
            pltpu.VMEM((nodes, FEAT), BF),
            pltpu.VMEM((nodes, FEAT), BF),
            matrix(FEAT),
            matrix(FEAT),
            matrix(3, FEAT // 4),
            matrix(2, FEAT // 4),
            matrix(FEAT // 2),
            matrix(FEAT // 2),
            matrix(3, FEAT // 8),
            matrix(2, FEAT // 8),
            pltpu.SemaphoreType.DMA((copies,)),
            pltpu.SemaphoreType.DMA((copies,)),
            pltpu.SemaphoreType.DMA((8,)),
            pltpu.SemaphoreType.DMA,
        ],
        compiler_params=pltpu.CompilerParams(
            collective_id=0, has_side_effects=True, vmem_limit_bytes=VMEM_BYTES
        ),
        name="layer",
    )(
        features.reshape(4, SIDE, FEAT), weight, tiles[0, 0], tile_coords[0, 0], tile_counts, cotangent,
    )
    return pl.pallas_call(
        deliver,
        out_shape=shapes,
        in_specs=[ANY, ANY, ANY],
        out_specs=(ANY, ANY, ANY),
        scratch_shapes=[pltpu.VMEM(shape.shape, shape.dtype) for shape in shapes]
        + [pltpu.SemaphoreType.DMA((3,)), pltpu.SemaphoreType.DMA((3,))],
        name="deliver",
    )(*results)


def solution(mesh):
    placed = (
        P(("col", "row"), None),
        P(),
        P("row", "col", None, None, None),
        P("row", "col", None, None),
        P("row", "col"),
        P(("row", "col"), None),
    )
    return jax.shard_map(
        local,
        mesh=mesh,
        in_specs=placed,
        out_specs=(P(("row", "col"), None), P(("col", "row"), None), P()),
        check_vma=False,
    )
```

```python
import functools

import jax
import jax.numpy as jnp
from jax import lax
from jax.experimental import pallas as pl
from jax.experimental.pallas import tpu as pltpu
from jax.sharding import PartitionSpec as P

MESH = pl.DeviceIdType.MESH
BF = jnp.bfloat16
F32 = jnp.float32
ANY = pl.BlockSpec(memory_space=pl.ANY)
VMEM = pl.BlockSpec(memory_space=pltpu.VMEM)
SMEM = pl.BlockSpec(memory_space=pltpu.SMEM)
VMEM_BYTES = 60 * 2**20
SIDE = 128
FEAT = 256
SLOTS = 384
PAIRS_FORWARD = (SLOTS + 64) // 2
PAIRS_BACK = (SLOTS + 32) // 2
CUTS = (0, 66, 132, 198, PAIRS_FORWARD)
STEPS = 2
PLACES = 512
H = (pl.ds(0, 2), pl.ds(2, 2))


class Group:
    def __init__(self, along):
        row = lax.axis_index("row")
        col = lax.axis_index("col")
        if along == "row":
            place = row
            self.device = lambda g: (g, col)
        else:
            place = lax.div(col, 2)
            core = lax.rem(col, 2)
            self.device = lambda g: (row, g * 2 + core)
            self.sibling = (row, place * 2 + 1 - core)
            self.core = core
        a = lax.div(place, 4)
        b = lax.rem(place, 4)
        up = lax.rem(b + 1, 4)
        down = lax.rem(b + 3, 4)
        far = lax.rem(b + 2, 4)
        self.own = place
        self.up, self.down, self.far = a * 4 + up, a * 4 + down, a * 4 + far
        self.other = (1 - a) * 4 + b
        self.other_up, self.other_down, self.other_far = (
            (1 - a) * 4 + up,
            (1 - a) * 4 + down,
            (1 - a) * 4 + far,
        )

    def peers(self):
        return [self.device(g) for g in (self.up, self.down, self.far, self.other)]


def greet(peers):
    barrier = pltpu.get_barrier_semaphore()
    for peer in peers:
        pl.semaphore_signal(barrier, inc=1, device_id=peer, device_id_type=MESH)
    pl.semaphore_wait(barrier, len(peers))


def ring_sum(group, send, whole, size, got, met, out, base):
    rows = lambda b: pl.ds(b * size, size)
    ring = [(group.device(g), lax.rem(g, 4)) for g in (group.up, group.down, group.far)]
    mine = lax.rem(group.own, 4)
    copies = [send(whole.at[rows(b)], got.at[k], peer) for k, (peer, b) in enumerate(ring)]
    yield
    for copy in copies:
        copy.wait_recv()
    met[0] = whole[rows(mine)] + got[0] + got[1] + got[2]
    copy = send(met.at[0], met.at[1], group.device(group.other))
    yield
    copy.wait_recv()
    spot = out.at[pl.ds(base + mine * size, size)]
    spot[...] = met[0] + met[1]
    copies = [send(spot, spot, peer) for peer, _ in ring]
    yield
    for copy in copies:
        copy.wait_recv()


def pair_then_ring_sum(group, send, whole, theirs, half, got, met, out):
    size = whole.shape[0] // 2
    mine = pl.ds(group.core * size, size)
    copy = send(whole.at[pl.ds((1 - group.core) * size, size)], theirs, group.sibling)
    yield
    copy.wait_recv()
    half[...] = whole[mine] + theirs[...]
    yield from ring_sum(group, send, half, size // 4, got, met, out, group.core * size)
    copy = send(out.at[mine], out.at[mine], group.sibling)
    yield
    copy.wait_recv()


def in_turn(tile_row):
    col = lax.axis_index("col")
    core, b, a = lax.rem(col, 2), lax.rem(lax.div(col, 2), 4), lax.div(col, 8)
    side = jnp.where((tile_row >> 5) == a, 4, 0)
    kin = jnp.where(((tile_row >> 2) & 1) == core, 8, 0)
    steps = (((tile_row >> 3) & 3) + 4 - b) & 3
    place = jnp.where(steps == 0, 3, jnp.where(steps == 1, 0, jnp.where(steps == 2, 2, 1)))
    return (kin + side + place) * 4 + (tile_row & 3)


class Sender:
    def __init__(self, send_sem, recv_sem):
        self.send_sem, self.recv_sem = send_sem, recv_sem
        self.used = 0
        self.all = []

    def __call__(self, src, dst, device):
        copy = pltpu.make_async_remote_copy(
            src_ref=src,
            dst_ref=dst,
            send_sem=self.send_sem.at[self.used],
            recv_sem=self.recv_sem.at[self.used],
            device_id=device,
            device_id_type=MESH,
        )
        self.used += 1
        self.all.append(copy)
        copy.start()
        return copy

    def finish(self):
        for copy in self.all:
            copy.wait_send()


def gather(group, send, own, spot, landed, tick=lambda: None, make=lambda h: None):
    up, down, other = (group.device(g) for g in (group.up, group.down, group.other))
    here = spot(group.own)
    c_up, c_down, c_other = [None, None], [None, None], [None, None]
    make(0)
    c_up[0] = send(own.at[H[0]], here.at[H[0]], up)
    c_other[0] = send(own.at[H[0]], here.at[H[0]], other)
    make(1)
    c_down[1] = send(own.at[H[1]], here.at[H[1]], down)
    c_up[1] = send(own.at[H[1]], here.at[H[1]], up)
    c_down[0] = send(own.at[H[0]], here.at[H[0]], down)
    c_other[1] = send(own.at[H[1]], here.at[H[1]], other)
    tick()
    f_up, f_down = [None, None], [None, None]
    c_up[0].wait_recv()
    far_first = send(spot(group.down).at[H[0]], spot(group.down).at[H[0]], up)
    landed(group.down, 0)
    c_down[1].wait_recv()
    far_second = send(spot(group.up).at[H[1]], spot(group.up).at[H[1]], down)
    landed(group.up, 1)
    for h in (0, 1):
        c_other[h].wait_recv()
        block = spot(group.other).at[H[h]]
        f_up[h] = send(block, block, up)
        f_down[h] = send(block, block, down)
        landed(group.other, h)
    tick()
    c_up[1].wait_recv()
    landed(group.down, 1)
    c_down[0].wait_recv()
    landed(group.up, 0)
    far_first.wait_recv()
    block = spot(group.far).at[H[0]]
    x_first = send(block, block, other)
    landed(group.far, 0)
    far_second.wait_recv()
    block = spot(group.far).at[H[1]]
    x_second = send(block, block, other)
    landed(group.far, 1)
    tick()
    for h in (0, 1):
        f_up[h].wait_recv()
        landed(group.other_down, h)
        f_down[h].wait_recv()
        landed(group.other_up, h)
    x_first.wait_recv()
    landed(group.other_far, 0)
    x_second.wait_recv()
    landed(group.other_far, 1)


def plus(target, *terms):
    total = terms[0][...].astype(F32)
    for term in terms[1:]:
        total = total + term[...].astype(F32)
    target[...] = total.astype(target.dtype)


def scatter_sum(group, send, ready, spot, got, tick=lambda: None):
    r1, r2d, r2u, r3, r4d, r4u, r5 = (got.at[k] for k in range(7))
    up, down, other = (group.device(g) for g in (group.up, group.down, group.other))
    ready(group.other_up)
    c2u = [send(spot(group.other_up).at[H[h]], r2d.at[H[h]], up) for h in (0, 1)]
    ready(group.other_down)
    c2d = [send(spot(group.other_down).at[H[h]], r2u.at[H[h]], down) for h in (0, 1)]
    ready(group.other_far)
    c1 = [send(spot(group.other_far).at[H[h]], r1.at[H[h]], other) for h in (0, 1)]
    ready(group.up)
    c4u, c4d = [None, None], [None, None]
    c4u[1] = send(spot(group.up).at[H[1]], r4d.at[H[1]], up)
    ready(group.down)
    c4d[0] = send(spot(group.down).at[H[0]], r4u.at[H[0]], down)
    ready(group.far)
    tick()
    c1[0].wait_recv()
    plus(r1.at[H[0]], r1.at[H[0]], spot(group.far).at[H[0]])
    c3u = send(r1.at[H[0]], r3.at[H[0]], up)
    tick()
    c1[1].wait_recv()
    plus(r1.at[H[1]], r1.at[H[1]], spot(group.far).at[H[1]])
    c3d = send(r1.at[H[1]], r3.at[H[1]], down)
    ready(group.other)
    tick()
    c5 = []
    for h in (0, 1):
        c2u[h].wait_recv()
        c2d[h].wait_recv()
        plus(r2d.at[H[h]], r2d.at[H[h]], r2u.at[H[h]], spot(group.other).at[H[h]])
        c5.append(send(r2d.at[H[h]], r5.at[H[h]], other))
        tick()
    c3u.wait_recv()
    plus(r3.at[H[0]], r3.at[H[0]], spot(group.up).at[H[0]])
    c4u[0] = send(r3.at[H[0]], r4d.at[H[0]], up)
    c3d.wait_recv()
    plus(r3.at[H[1]], r3.at[H[1]], spot(group.down).at[H[1]])
    c4d[1] = send(r3.at[H[1]], r4u.at[H[1]], down)
    ready(group.own)
    for copies in (c5, c4u, c4d):
        for copy in copies:
            copy.wait_recv()
    return (spot(group.own), r4d, r4u, r5)


def pair_list(key, source, live, outs, empty, pairs):
    def iota(shape, dim):
        return lax.broadcasted_iota(jnp.int32, shape, dim)

    def add(x, axis):
        return jnp.sum(x, axis=axis, keepdims=True, dtype=jnp.int32)

    def upright(x):
        n = x.shape[1]
        return add(jnp.where(iota((n, n), 0) == iota((n, n), 1), x, 0), 1)

    key_up, source_up, live_up = upright(key), upright(source), upright(live)
    square = (SLOTS, SLOTS)
    before = (key_up == key) & (iota(square, 1) < iota(square, 0))
    rank = add(jnp.where(before, live, 0), 1)
    member = jnp.where(key_up == iota((SLOTS, SIDE), 1), live_up, 0)
    held = (add(member, 0) + 1) >> 1
    tri = (SIDE, SIDE)
    start = add(jnp.where(iota(tri, 0) < iota(tri, 1), upright(held), 0), 0)
    place = jnp.where(live_up > 0, 2 * add(member * start, 1) + rank, -1)
    wide = (SLOTS, PLACES)
    hit = place == iota(wide, 1)
    slots = add(jnp.where(hit, iota(wide, 0), 0), 0)
    sources = add(jnp.where(hit, source_up - empty, 0), 0) + empty
    firsts = add(jnp.where(hit & (rank == 0), 1, 0), 0)
    last = jnp.where(held > 0, start + held - 1, pairs)
    last = jnp.concatenate([last, jnp.zeros((1, PLACES - SIDE), jnp.int32)], axis=1)
    row = iota((8, PLACES), 0)
    return jnp.where(row == 0, slots, jnp.where(row == 1, sources, jnp.where(row == 2, firsts, last)))


def tile_step(transpose, table, tiles, panel, sums, q, run):
    values = [tiles[table[0, 2 * q + k]] for k in (0, 1)]
    sources = [panel[table[1, 2 * q + k]] for k in (0, 1)]
    left, right = jnp.concatenate(values, 0 if transpose else 1), jnp.concatenate(sources, 0)
    run = jnp.where(table[2, 2 * q] == 1, 0.0, run)
    run = run + lax.dot_general(
        left, right, (((0 if transpose else 1,), (0,)), ((), ())), preferred_element_type=F32
    )
    sums[q] = run.astype(BF)
    return run


def tile_sums(transpose, table, tiles, panel, sums, first, last, run, steps):
    unroll = (last - first) // steps

    def several(i, run):
        for u in range(unroll):
            run = tile_step(transpose, table, tiles, panel, sums, first + i * unroll + u, run)
        return run

    return lax.fori_loop(0, steps, several, run)


def layer(
    features, weight_hbm, tiles_hbm, coords, count, cotangent_hbm,
    output_hbm, feature_hbm, weight_grad_hbm,
    tiles, panel, grads, sums_forward, sums_back, given, theirs, back, got_forward, got_back,
    lists, table_forward, table_back, weight, cotangent, output, feature_grad, weight_grad,
    total_hi, total_lo, own, whole, row_sum, row_got, row_met, half, half_got, col_got, col_met,
    send_sem, recv_sem, load_sem, tile_sem,
):
    rows_group, cols_group = Group("row"), Group("col")
    core, sibling = cols_group.core, cols_group.sibling
    greet(rows_group.peers() + cols_group.peers() + [sibling])
    send = Sender(send_sem, recv_sem)
    loads = [
        pltpu.make_async_copy(features, panel.at[pl.ds(rows_group.own * 4, 4)], load_sem.at[0]),
        pltpu.make_async_copy(weight_hbm, weight, load_sem.at[1]),
        pltpu.make_async_copy(cotangent_hbm, cotangent, load_sem.at[2]),
    ]
    tile_load = pltpu.make_async_copy(tiles_hbm, tiles, tile_sem)
    table_loads = [
        pltpu.make_async_copy(lists.at[0], table_forward, load_sem.at[3]),
        pltpu.make_async_copy(lists.at[1], table_back, load_sem.at[4]),
    ]

    def prepare():
        for copy in loads:
            copy.start()
        tile_load.start()
        panel[32] = jnp.zeros((SIDE, FEAT), BF)
        grads[64] = jnp.zeros((SIDE, FEAT), BF)
        tile_row, tile_col = coords[0:1], coords[1:2]
        live = jnp.where(
            lax.broadcasted_iota(jnp.int32, (1, SLOTS), 1) < count[0, 0], 1, 0
        )
        lists[0] = pair_list(in_turn(tile_row), tile_col, live, 64, 32, PAIRS_FORWARD)
        lists[1] = pair_list(tile_col, tile_row, live, 32, 64, PAIRS_BACK)
        for copy in table_loads:
            copy.start()
        yield

    first = prepare()
    gather(
        rows_group, send, features, lambda g: panel.at[pl.ds(g * 4, 4)], lambda g, h: None,
        lambda: next(first, None),
    )
    for copy in loads + table_loads:
        copy.wait()
    tile_load.wait()
    group = cols_group
    order = (
        group.other_up, group.other_down, group.other_far, group.other,
        group.up, group.down, group.far, group.own,
    )
    held = {id(g): k for k, g in enumerate(order)}
    pairs = []

    def give(k):
        for t in range(4):
            given[k, t] = sums_forward[table_forward[3, k * 4 + t]]
        pairs.append(send(given.at[k], theirs.at[k], sibling))

    block = (SIDE, FEAT)
    sums_forward[PAIRS_FORWARD] = jnp.zeros(block, BF)
    run = jnp.zeros(block, F32)
    for k, (begin, end) in enumerate(zip(CUTS[:-1], CUTS[1:])):
        run = tile_sums(
            False, table_forward, tiles, panel, sums_forward, begin, end, run, 2
        )
        if k < 3:
            give(k)
    for k in range(3, 8):
        give(k)

    def ready(g):
        k = held[id(g)]
        pairs[k].wait_recv()
        for t in range(4):
            mine = sums_forward[table_forward[3, (k + 8) * 4 + t]]
            theirs[k, t] = (theirs[k, t].astype(F32) + mine.astype(F32)).astype(BF)

    terms = scatter_sum(group, send, ready, lambda g: theirs.at[held[id(g)]], got_forward)
    def make(h):
        for t in (2 * h, 2 * h + 1):
            total = terms[0][t].astype(F32)
            for term in terms[1:]:
                total = total + term[t].astype(F32)
            rows = pl.ds(t * SIDE, SIDE)
            high = total.astype(BF)
            low = (total - high.astype(F32)).astype(BF)
            total_hi[rows] = high
            total_lo[rows] = low
            hidden = jnp.dot(high, weight[...], preferred_element_type=F32) + jnp.dot(
                low, weight[...], preferred_element_type=F32
            )
            sigma = 1.0 / (1.0 + jnp.exp(-hidden))
            output[rows] = (hidden * sigma).astype(BF)
            slope = (cotangent[rows].astype(F32) * sigma * (1.0 + hidden * (1.0 - sigma))).astype(BF)
            own[rows] = slope
            grads[group.own * 8 + core * 4 + t] = lax.dot_general(
                slope, weight[...], (((1,), (1,)), ((), ())), preferred_element_type=F32
            ).astype(BF)
        landed(group.own, h)

    def spot(g):
        return grads.at[pl.ds((g * 2 + core) * 4, 4)]

    def landed(g, h):
        block = spot(g).at[H[h]]
        shared.append(send(block, block, sibling))

    output_copy = pltpu.make_async_copy(output, output_hbm, load_sem.at[5])

    def weight_sum():
        output_copy.start()
        over = (((0,), (0,)), ((), ()))
        whole[...] = lax.dot_general(
            total_hi[...], own[...], over, preferred_element_type=F32
        ) + lax.dot_general(total_lo[...], own[...], over, preferred_element_type=F32)
        yield from ring_sum(rows_group, send, whole, FEAT // 4, row_got, row_met, row_sum, 0)

    shared = []
    stages = weight_sum()
    gather(group, send, spot(group.own), spot, landed, lambda: next(stages, None), make)
    for _ in stages:
        pass
    for copy in shared:
        copy.wait_recv()
    sums_back[PAIRS_BACK] = jnp.zeros(block, BF)
    tile_sums(
        True, table_back, tiles, grads, sums_back, 0, PAIRS_BACK, jnp.zeros(block, F32), STEPS
    )

    def gathered(g):
        for t in range(4):
            back[g * 4 + t] = sums_back[table_back[3, g * 4 + t]]

    stages = pair_then_ring_sum(
        cols_group, send, row_sum, half_got, half, col_got, col_met, weight_grad
    )
    terms = scatter_sum(
        rows_group, send, gathered, lambda g: back.at[pl.ds(g * 4, 4)], got_back, lambda: next(stages, None)
    )
    for t in range(4):
        total = terms[0][t].astype(F32)
        for term in terms[1:]:
            total = total + term[t].astype(F32)
        feature_grad[pl.ds(t * SIDE, SIDE)] = total.astype(BF)
    feature_copy = pltpu.make_async_copy(feature_grad, feature_hbm, load_sem.at[6])
    feature_copy.start()
    for _ in stages:
        pass
    weight_copy = pltpu.make_async_copy(weight_grad, weight_grad_hbm, load_sem.at[7])
    weight_copy.start()
    send.finish()
    output_copy.wait()
    feature_copy.wait()
    weight_copy.wait()


def deliver(*refs):
    count = (len(refs) - 2) // 3
    into, out = refs[-2], refs[-1]
    sources, targets, held = refs[:count], refs[count : 2 * count], refs[2 * count : 3 * count]
    first = [pltpu.make_async_copy(sources[k], held[k], into.at[k]) for k in range(count)]
    second = [pltpu.make_async_copy(held[k], targets[k], out.at[k]) for k in range(count)]
    for copy in first:
        copy.start()
    for k in range(count):
        first[k].wait()
        second[k].start()
    for copy in second:
        copy.wait()


def local(features, weight, tiles, tile_coords, tile_counts, cotangent):
    nodes = 4 * SIDE
    blocks = lambda *lead: pltpu.VMEM(lead + (SIDE, FEAT), BF)
    matrix = lambda *shape: pltpu.VMEM(shape + (FEAT,), F32)
    copies = 14 + 8 + 14 + 16 + 14 + 7 + 14 + 9
    shapes = (
        jax.ShapeDtypeStruct((nodes, FEAT), BF),
        jax.ShapeDtypeStruct((nodes, FEAT), BF),
        jax.ShapeDtypeStruct((FEAT, FEAT), F32),
    )
    results = pl.pallas_call(
        layer,
        out_shape=shapes,
        in_specs=[ANY, ANY, ANY, VMEM, SMEM, ANY],
        out_specs=(ANY, ANY, ANY),
        scratch_shapes=[
            pltpu.VMEM((SLOTS, SIDE, SIDE), BF),
            blocks(33),
            blocks(65),
            blocks(PAIRS_FORWARD + 1),
            blocks(PAIRS_BACK + 1),
            blocks(8, 4),
            blocks(8, 4),
            blocks(32),
            blocks(7, 4),
            blocks(7, 4),
            pltpu.VMEM((2, 8, PLACES), jnp.int32),
            pltpu.SMEM((8, PLACES), jnp.int32),
            pltpu.SMEM((8, PLACES), jnp.int32),
            pltpu.VMEM((FEAT, FEAT), BF),
            pltpu.VMEM((nodes, FEAT), BF),
            pltpu.VMEM((nodes, FEAT), BF),
            pltpu.VMEM((nodes, FEAT), BF),
            matrix(FEAT),
            pltpu.VMEM((nodes, FEAT), BF),
            pltpu.VMEM((nodes, FEAT), BF),
            pltpu.VMEM((nodes, FEAT), BF),
            matrix(FEAT),
            matrix(FEAT),
            matrix(3, FEAT // 4),
            matrix(2, FEAT // 4),
            matrix(FEAT // 2),
            matrix(FEAT // 2),
            matrix(3, FEAT // 8),
            matrix(2, FEAT // 8),
            pltpu.SemaphoreType.DMA((copies,)),
            pltpu.SemaphoreType.DMA((copies,)),
            pltpu.SemaphoreType.DMA((8,)),
            pltpu.SemaphoreType.DMA,
        ],
        compiler_params=pltpu.CompilerParams(
            collective_id=0, has_side_effects=True, vmem_limit_bytes=VMEM_BYTES
        ),
        name="layer",
    )(
        features.reshape(4, SIDE, FEAT), weight, tiles[0, 0], tile_coords[0, 0], tile_counts, cotangent,
    )
    return pl.pallas_call(
        deliver,
        out_shape=shapes,
        in_specs=[ANY, ANY, ANY],
        out_specs=(ANY, ANY, ANY),
        scratch_shapes=[pltpu.VMEM(shape.shape, shape.dtype) for shape in shapes]
        + [pltpu.SemaphoreType.DMA((3,)), pltpu.SemaphoreType.DMA((3,))],
        name="deliver",
    )(*results)


def solution(mesh):
    placed = (
        P(("col", "row"), None),
        P(),
        P("row", "col", None, None, None),
        P("row", "col", None, None),
        P("row", "col"),
        P(("row", "col"), None),
    )
    return jax.shard_map(
        local,
        mesh=mesh,
        in_specs=placed,
        out_specs=(P(("row", "col"), None), P(("col", "row"), None), P()),
        check_vma=False,
    )
```
